128 devices in a mesh: state: 32 (over z, x, core), rank: 4 (over y).
Axes of the slice: x: 4, y: 4, z: 4, core: 2. Of those that a mesh axis runs over, the one named last changes fastest.
Arguments:
- token_ids: int32 [3, 128], replicated, may hold values from 0 to 9999
- word_emb: bfloat16 [10000, 128], replicated, may hold values from -6 to 6
- state_emb: bfloat16 [131072, 128], P('state'), may hold values from -3 to 3
- log_norm: float32 [131072], P('state'), may hold values from -0.5 to 1
- beta_last: bfloat16 [131072, 128], P('state'), may hold values from 0.19921875 to 5
- forward_marg: bfloat16 [131072, 384], P('state'), may hold values from 0.049804688 to 2
- trans_left: bfloat16 [131072, 2048], P('state', 'rank'), as said below
- trans_right: bfloat16 [131072, 2048], P('state', 'rank'), as said below
Outputs:
- beta_first: bfloat16 [131072, 128], P('state')
- grad_left: bfloat16 [131072, 2048], P('state', 'rank')
- grad_right: bfloat16 [131072, 2048], P('state', 'rank')
The draws below stay inside these ranges and needn't reach their ends.
Inputs may be any that keep to these rules, and one draw needn't show every extreme that they name: `trans_left`: positive entries. `trans_right`: positive entries.
All inputs are finite; a program needn't handle non-finite values.
Results may differ from the reference program's by a relative error of at most 0.009.
Values may be sent and summed in bfloat16 or wider, within the bound.
A program may use at most 128 MiB of HBM per device.

```python
import math
import jax
import jax.numpy as jnp
import numpy as np
from jax import lax

R = 2048
H = 128
VOCAB = 10000
B = 128
STEPS = 3
S = 131072


def cluster_ids(key):
    groups = max(S // 512, 8)
    labels = jax.random.randint(jax.random.fold_in(key, 5), (S,), 0, groups)
    return (labels, groups)


def column_factor(key, labels, groups):
    table = jax.random.normal(key, (groups, R), jnp.float32)
    return jnp.exp(2.0 * jnp.take(table, labels, axis=0) - 2.0)


def draw_state_emb(key, part):
    labels, groups = cluster_ids(key)
    key = jax.random.fold_in(key, 37)
    first, second = jax.random.split(key)
    centers = jnp.clip(jax.random.normal(second, (groups, H), jnp.float32), -4.0, 4.0)
    noise = jnp.clip(jax.random.normal(first, (S, H), jnp.float32), -4.0, 4.0)
    values = (1.5 * jnp.take(centers, labels, axis=0) + noise) / math.sqrt(H)
    return values.astype(jnp.bfloat16)


def draw_trans_left(key, part):
    labels, groups = cluster_ids(key)
    key = jax.random.fold_in(key, 11)
    first = jax.random.fold_in(key, 0)
    third = jax.random.fold_in(key, 2)
    noise = jax.random.normal(first, (S, R), jnp.float32)
    rising = 1.0 + 2.0 * jnp.arange(S, dtype=jnp.float32)[:, None] / S
    factor = column_factor(third, labels, groups)
    return (jnp.exp(2.0 * noise - 2.0) * factor * rising).astype(jnp.bfloat16)


def draw_trans_right(key, part):
    labels, groups = cluster_ids(key)
    key = jax.random.fold_in(key, 23)
    first = jax.random.fold_in(key, 0)
    third = jax.random.fold_in(key, 2)
    noise = jax.random.normal(first, (S, R), jnp.float32)
    factor = column_factor(third, labels, groups)
    return (jnp.exp(2.0 * noise - 2.0) * factor / S).astype(jnp.bfloat16)


def touch_ends(drawn, own_key, least, high):
    longest = drawn.shape.index(max(drawn.shape))
    spots = []
    for shift in (0, 1):
        where = [jax.random.randint(jax.random.fold_in(own_key, axis), (), 0, length) for axis, length in enumerate(drawn.shape)]
        where[longest] = (where[longest] + shift) % drawn.shape[longest]
        spots.append(tuple(where))
    return drawn.at[spots[0]].set(least).at[spots[1]].set(high)


def level_of(own_key, dims, shards, smallest, high):
    def one(position, blocks):
        draws = jax.random.uniform(jax.random.fold_in(jax.random.fold_in(own_key, 6), position), (blocks,), jnp.float32, smallest / len(shards), high / len(shards))
        return jnp.repeat(jnp.exp(draws), dims[position] // blocks).reshape((-1,) + (1,) * (len(dims) - position - 1))

    factor_of = one(*shards[0])
    for cut in shards[1:]:
        factor_of = factor_of * one(*cut)
    return factor_of


def rank_table(amount, skew):
    loads = [(1 << 20) // math.isqrt(grade ** skew) + 1 for grade in range(1, amount + 1)]
    spread = 1 + sum(loads) // (1 << 30)
    return np.cumsum(np.array([max(1, weight // spread) for weight in loads]))


def skewed_ids(own_key, extent, amount, skew):
    listing = rank_table(amount, skew)
    lot = jax.random.randint(jax.random.fold_in(own_key, 1), extent, 0, int(listing[amount - 1]))
    rank = jnp.searchsorted(jnp.asarray(listing, jnp.int32), lot, side="right")
    return jax.random.permutation(jax.random.fold_in(own_key, 2), amount)[rank].astype(jnp.int32)


def normal_values(stream_key, shape, width, limit, kind=jnp.bfloat16):
    entries = width * jax.random.normal(stream_key, shape, jnp.float32)
    return jnp.clip(entries, min=-limit, max=limit).astype(kind)


def setup_inputs(seed: int = 0) -> dict:
    keys = jax.random.split(jax.random.key(seed), 9)
    token_ids = touch_ends(skewed_ids(keys[0], (STEPS, B), VOCAB, 2), jax.random.fold_in(keys[0], 3), 0, VOCAB - 1).astype(jnp.int32)
    word_emb = normal_values(keys[1], (VOCAB, H), 1.0, 6.0)
    state_emb = draw_state_emb(jax.random.fold_in(keys[8], 71), 0)
    log_norm = jnp.clip(-0.5 + 1.5 * jax.random.uniform(keys[3], (S,), jnp.float32) ** level_of(keys[3], (S,), ((0, 32),), -0.2, 0.2), -0.5, 1.0)
    beta_last = jnp.clip(jnp.exp(math.log(5.0) - 3.2227897 * jax.random.uniform(keys[4], (S, B), jnp.float32) ** level_of(keys[4], (S, B), ((0, 32),), -0.2, 0.2)), 0.19921875, 5.0).astype(jnp.bfloat16)
    forward_marg = jnp.clip(jnp.exp(math.log(2.0) - 3.6927934 * jax.random.uniform(keys[5], (S, STEPS * B), jnp.float32) ** level_of(keys[5], (S, STEPS * B), ((0, 32),), -0.2, 0.2)), 0.049804688, 2.0).astype(jnp.bfloat16)
    trans_left = draw_trans_left(jax.random.fold_in(keys[8], 71), 0)
    trans_right = draw_trans_right(jax.random.fold_in(keys[8], 71), 0)
    return {"token_ids": token_ids, "word_emb": word_emb, "state_emb": state_emb, "log_norm": log_norm, "beta_last": beta_last, "forward_marg": forward_marg, "trans_left": trans_left, "trans_right": trans_right}


def reference(token_ids, word_emb, state_emb, log_norm, beta_last, forward_marg, trans_left, trans_right):
    beta = beta_last
    weighted_list = []
    proj_list = []
    for step in reversed(range(STEPS)):
        words = jnp.take(word_emb, token_ids[step], axis=0)
        logits = jnp.dot(state_emb, words.T, preferred_element_type=jnp.float32)
        emit = jnp.exp(logits - log_norm[:, None])
        weighted = (emit * beta.astype(jnp.float32)).astype(jnp.bfloat16)
        proj = lax.dot_general(weighted, trans_right, (((0,), (0,)), ((), ())), preferred_element_type=jnp.float32)
        projb = proj.astype(jnp.bfloat16)
        raw = lax.dot_general(trans_left, projb, (((1,), (1,)), ((), ())), preferred_element_type=jnp.float32)
        mass = jnp.sum(raw, axis=0) / S
        beta = (raw / mass[None, :]).astype(jnp.bfloat16)
        weighted_list.insert(0, weighted)
        proj_list.insert(0, projb)
    weighted_all = jnp.concatenate(weighted_list, axis=1)
    proj_all = jnp.concatenate(proj_list, axis=0)
    fwd_proj = lax.dot_general(forward_marg, trans_left, (((0,), (0,)), ((), ())), preferred_element_type=jnp.float32)
    fwd_proj = (fwd_proj / S).astype(jnp.bfloat16)
    count = STEPS * B
    grad_left = (jnp.dot(forward_marg, proj_all, preferred_element_type=jnp.float32) / count).astype(jnp.bfloat16)
    grad_right = (jnp.dot(weighted_all, fwd_proj, preferred_element_type=jnp.float32) / count).astype(jnp.bfloat16)
    return beta, grad_left, grad_right
```

```python
import functools

import jax
import jax.numpy as jnp
from jax import lax
from jax.experimental import pallas as pl
from jax.experimental.pallas import tpu as pltpu
from jax.sharding import PartitionSpec as P

MESH = pl.DeviceIdType.MESH
F32 = jnp.float32
BF16 = jnp.bfloat16
GROUP = 8
RANKS = 4
BLOCKS = 2 * RANKS
HALVES = 2
STEPS = 3


def nn(a, b):
    return lax.dot_general(a, b, (((1,), (0,)), ((), ())), preferred_element_type=F32)


def nt(a, b):
    return lax.dot_general(a, b, (((1,), (1,)), ((), ())), preferred_element_type=F32)


def recursion(
    states_all, zs,
    ids, word_emb, semb, ln, beta, fm, left, right,
    wn_o, pb_o, fw_o, bt_o,
    ids_v, emb_v, semb_v, ln_v, beta_v, fm_v, u_v, v_v,
    words, w, wn, emit, acc, keep, csm, pb,
    sb1, rb1, rb2, pj, fs1, fr1, fr2, fj, cs, cr1, cr2,
    rs_s, rs_r, ms, mr,
    load, store, s1s, s1r, s2s, s2r, s3s, s3r, f1s, f1r, f2s, f2r, f3s, f3r, cs_s, cs_r,
    rss, rsr, ags, agr, mss, msr,
):
    state = lax.axis_index("state")
    y = lax.axis_index("rank")
    g = lax.rem(state, GROUP)
    z = state // GROUP
    yp, yo, ym = lax.rem(y + 1, RANKS), lax.rem(y + 2, RANKS), lax.rem(y + 3, RANKS)
    vocab, hidden = word_emb.shape
    padded = emb_v.shape[0]
    local, ranks = left.shape
    blk = local // BLOCKS
    hb = w.shape[3]
    batch = HALVES * hb
    half_ranks = ranks // 2

    loads = [
        (ids, ids_v), (word_emb, emb_v.at[pl.ds(0, vocab)]), (semb, semb_v), (ln, ln_v), (beta, beta_v),
        (right, v_v), (left, u_v), (fm, fm_v),
    ]
    loads = [pltpu.make_async_copy(src, dst, load.at[k]) for k, (src, dst) in enumerate(loads)]
    for copy in loads:
        copy.start()
    ids_l, emb_l, semb_l, ln_l, beta_l, v_l, u_l, fm_l = loads

    def group_peer(d):
        p = lax.rem(g + d, GROUP)
        return p, (z * GROUP + p, y)

    def z_peer(d):
        return (lax.rem(z + d, zs) * GROUP + g, y)

    barrier = pltpu.get_barrier_semaphore()
    greeted = [group_peer(d)[1] for d in range(1, GROUP)] + [z_peer(d) for d in range(1, zs)]
    greeted += [(state, other) for other in (yp, yo, ym)]
    for who in greeted:
        pl.semaphore_signal(barrier, inc=1, device_id=who, device_id_type=MESH)

    def send(src, dst, send_sem, recv_sem, who):
        pltpu.make_async_remote_copy(
            src_ref=src, dst_ref=dst, send_sem=send_sem, recv_sem=recv_sem, device_id=who, device_id_type=MESH
        ).start()

    def await_bytes(ref, sem):
        pltpu.make_async_copy(ref, ref, sem).wait()

    def rows(ref, j):
        return ref[pl.ds(pl.multiple_of(j * blk, blk), blk), :]

    emb_v[pl.ds(vocab, padded - vocab), :] = jnp.zeros((padded - vocab, hidden), BF16)
    chunk = 1024

    def find_words(t, column):
        def one(c, total):
            lane = lax.broadcasted_iota(jnp.int32, (batch, chunk), 1) + c * chunk
            hot = jnp.where(lane.astype(F32) == column, 1.0, 0.0).astype(BF16)
            return total + nn(hot, emb_v[pl.ds(pl.multiple_of(c * chunk, chunk), chunk), :])

        total = lax.fori_loop(0, padded // chunk, one, jnp.zeros((batch, hidden), F32))
        words[t] = total.astype(BF16)

    ids_l.wait()
    id_rows = jnp.concatenate([ids_v[...].astype(F32), jnp.zeros((8 - STEPS, batch), F32)], axis=0)
    id_cols = id_rows.T
    emb_l.wait()
    find_words(STEPS - 1, id_cols[:, STEPS - 1:STEPS])

    semb_l.wait()
    ln_l.wait()
    beta_l.wait()
    v_l.wait()
    eye = jnp.where(
        lax.broadcasted_iota(jnp.int32, (batch, batch), 0) == lax.broadcasted_iota(jnp.int32, (batch, batch), 1), 1.0, 0.0
    ).astype(BF16)

    def first(j, total):
        logits = nt(words[STEPS - 1], rows(semb_v, j))
        em = jnp.exp(logits - ln_v[j])
        wt = (em * nt(eye, rows(beta_v, j))).astype(BF16)
        for h in range(HALVES):
            w[0, h, j] = wt[h * hb:(h + 1) * hb]
        return total + nn(wt, rows(v_v, j))

    total = lax.fori_loop(0, BLOCKS, first, jnp.zeros((batch, ranks), F32))
    for h in range(HALVES):
        acc[h] = total[h * hb:(h + 1) * hb]

    pl.semaphore_wait(barrier, len(greeted))

    def sum1(i, h):
        part = acc[h].astype(BF16)
        for p in range(GROUP):
            r, c = 16 * (p % 4), half_ranks * (p // 4)
            sb1[i, h, p] = part[r:r + 16, c:c + half_ranks]
        for d in range(1, GROUP):
            p, who = group_peer(d)
            send(sb1.at[i, h, p], rb1.at[i, h, d - 1], s1s.at[i, h], s1r.at[i, h], who)

    def sum2(i, h):
        await_bytes(rb1.at[i, h], s1r.at[i, h])
        total = sb1[i, h, g].astype(F32)
        for d in range(GROUP - 1):
            total += rb1[i, h, d].astype(F32)
        rb2[i, h, z] = total.astype(BF16)
        for d in range(1, zs):
            send(rb2.at[i, h, z], rb2.at[i, h, z], s2s.at[i, h], s2r.at[i, h], z_peer(d))

    def sum3(i, h):
        await_bytes(rb2.at[i, h, pl.ds(0, zs - 1)], s2r.at[i, h])
        total = rb2[i, h, 0].astype(F32)
        for d in range(1, zs):
            total += rb2[i, h, d].astype(F32)
        pj[i, h, g] = total.astype(BF16)
        for d in range(1, GROUP):
            send(pj.at[i, h, g], pj.at[i, h, g], s3s.at[i, h], s3r.at[i, h], group_peer(d)[1])

    def fwd1(i):
        t = STEPS - 1 - i

        def one(j, total):
            cols = fm_v[pl.ds(pl.multiple_of(j * blk, blk), blk), pl.ds(pl.multiple_of(t * batch, batch), batch)]
            return total + nn(cols.T, rows(u_v, j))

        total = lax.fori_loop(0, BLOCKS, one, jnp.zeros((batch, ranks), F32))
        for p in range(GROUP):
            fs1[i, p] = total[16 * p:16 * p + 16].astype(BF16)
        for d in range(1, GROUP):
            p, who = group_peer(d)
            send(fs1.at[i, p], fr1.at[i, d - 1], f1s.at[i], f1r.at[i], who)

    def fwd2(i):
        await_bytes(fr1.at[i], f1r.at[i])
        total = fs1[i, g].astype(F32)
        for d in range(GROUP - 1):
            total += fr1[i, d].astype(F32)
        fr2[i, z] = total.astype(BF16)
        for d in range(1, zs):
            send(fr2.at[i, z], fr2.at[i, z], f2s.at[i], f2r.at[i], z_peer(d))

    def fwd3(i):
        await_bytes(fr2.at[i, pl.ds(0, zs - 1)], f2r.at[i])
        total = fr2[i, 0].astype(F32)
        for d in range(1, zs):
            total += fr2[i, d].astype(F32)
        fj[i, g] = (total / states_all).astype(BF16)
        for d in range(1, GROUP):
            send(fj.at[i, g], fj.at[i, g], f3s.at[i], f3r.at[i], group_peer(d)[1])

    tiles = ranks // 128

    def columns1():
        def one(j, total):
            return total + nn(jnp.ones((16, blk), BF16), rows(u_v, j))

        total = lax.fori_loop(0, BLOCKS, one, jnp.zeros((16, ranks), F32))
        cs[...] = jnp.zeros_like(cs)
        for c in range(tiles):
            cs[0, c:c + 1, :] = total[0:1, 128 * c:128 * c + 128]
        for d in range(1, GROUP):
            send(cs.at[0], cr1.at[d - 1], cs_s.at[0], cs_r.at[0], group_peer(d)[1])

    def columns2():
        await_bytes(cr1, cs_r.at[0])
        total = cs[0]
        for d in range(GROUP - 1):
            total += cr1[d]
        cs[1] = total
        for d in range(1, zs):
            send(cs.at[1], cr2.at[d - 1], cs_s.at[1], cs_r.at[1], z_peer(d))

    def columns3():
        await_bytes(cr2, cs_r.at[1])
        total = cs[1]
        for d in range(zs - 1):
            total += cr2[d]
        line = jnp.concatenate([total[c:c + 1] for c in range(tiles)], axis=1)
        high = line.astype(BF16)
        rest = line - high.astype(F32)
        mid = rest.astype(BF16)
        low = (rest - mid.astype(F32)).astype(BF16)
        parts = [x.astype(F32) for x in (high, mid, low)] + [jnp.zeros((13, ranks), F32)]
        csm[...] = jnp.concatenate(parts, axis=0).astype(BF16)

    def raw(i, h):
        await_bytes(pj.at[i, h, pl.ds(0, GROUP - 1)], s3r.at[i, h])
        for p in range(GROUP):
            r, c = 16 * (p % 4), half_ranks * (p // 4)
            pb[i, h, r:r + 16, c:c + half_ranks] = pj[i, h, p]
        proj = pb[i, h]
        for k, (j, who) in enumerate(((2 * yo, yp), (2 * yo + 1, ym), (2 * yp + 1, yp), (2 * ym, ym))):
            rs_s[i, h, k] = nt(proj, rows(u_v, j)).astype(BF16)
            send(rs_s.at[i, h, k], rs_r.at[i, h, k], rss.at[i, h, k], rsr.at[i, h, k], (state, who))
        part = nt(csm[...], proj)
        ms[i, h, 0:1, 0:hb] = part[0:1] + part[1:2] + part[2:3]
        for d, who in enumerate((yp, yo, ym)):
            send(ms.at[i, h], mr.at[i, h, d], mss.at[i, h], msr.at[i, h], (state, who))
        for k, j in enumerate((2 * yp, 2 * ym + 1, 2 * y, 2 * y + 1)):
            keep[h, k] = nt(proj, rows(u_v, j))

    def relay(i, h):
        for k, who in ((0, yp), (1, ym)):
            await_bytes(rs_r.at[i, h, k], rsr.at[i, h, k])
            rs_s[i, h, 4 + k] = (keep[h, k] + rs_r[i, h, k].astype(F32)).astype(BF16)
            send(rs_s.at[i, h, 4 + k], rs_r.at[i, h, 4 + k], rss.at[i, h, 4 + k], rsr.at[i, h, 4 + k], (state, who))

    def gather(i, h, k, j, who):
        send(w.at[i + 1, h, j], w.at[i + 1, h, j], ags.at[i, h, k], agr.at[i, h, k], (state, who))

    def own(i, h):
        await_bytes(mr.at[i, h], msr.at[i, h])
        mass = ms[i, h] + mr[i, h, 0] + mr[i, h, 1] + mr[i, h, 2]
        mass = mass.T[0:hb, 0:1] / states_all
        for part, (a, b, who) in enumerate(((3, 4, yp), (2, 5, ym))):
            for k in (a, b):
                await_bytes(rs_r.at[i, h, k], rsr.at[i, h, k])
            total = keep[h, 2 + part] + rs_r[i, h, a].astype(F32) + rs_r[i, h, b].astype(F32)
            new = (total / mass).astype(BF16).astype(F32)
            w[i + 1, h, 2 * y + part] = (emit[i, h, part] * new).astype(BF16)
            gather(i, h, part, 2 * y + part, who)
        gather(i, h, 2, 2 * y + 1, yp)
        gather(i, h, 3, 2 * y, ym)

    def landed(i, h, k):
        j = (2 * ym, 2 * yp + 1, 2 * ym + 1, 2 * yp, 2 * yo, 2 * yo + 1)[k]
        await_bytes(w.at[i + 1, h, j], agr.at[i, h, k])
        return j

    def forward(i, h):
        gather(i, h, 4, landed(i, h, 0), yp)
        gather(i, h, 5, landed(i, h, 1), ym)

    def project(i, h):
        def term(j):
            return nn(w[i, h, j], rows(v_v, j))

        total = term(2 * y) + term(2 * y + 1) + term(2 * ym) + term(2 * yp + 1)
        for k in range(2, 6):
            total += term(landed(i - 1, h, k))
        acc[h] = total

    def turn(i):
        t = STEPS - 1 - i

        def one(j, carry):
            both = jnp.concatenate([w[i, h, j] for h in range(HALVES)], axis=0)
            wn[pl.ds(pl.multiple_of(j * blk, blk), blk), pl.ds(pl.multiple_of(t * batch, batch), batch)] = both.T
            return carry

        lax.fori_loop(0, BLOCKS, one, 0)

    for h in range(HALVES):
        sum1(0, h)
    u_l.wait()
    columns1()
    sum2(0, 0)
    sum2(0, 1)
    columns2()

    ms[...] = jnp.zeros_like(ms)
    for t in range(STEPS - 1):
        find_words(t, id_cols[:, t:t + 1])
    for i in range(STEPS - 1):
        for part in range(2):
            logits = nt(words[STEPS - 2 - i], rows(semb_v, 2 * y + part))
            em = jnp.exp(logits - ln_v[2 * y + part])
            for h in range(HALVES):
                emit[i, h, part] = em[h * hb:(h + 1) * hb]
    emit[STEPS - 1] = jnp.ones_like(emit[STEPS - 1])
    sum3(0, 0)
    sum3(0, 1)
    columns3()
    fm_l.wait()

    a, b = 0, 1

    def body(i, carry):
        more = i < STEPS - 1
        raw(i, a)

        @pl.when(i > 0)
        def _():
            project(i, b)
            sum1(i, b)

        relay(i, a)

        @pl.when(i > 0)
        def _():
            sum2(i, b)

        fwd1(i)
        own(i, a)

        @pl.when(i > 0)
        def _():
            sum3(i, b)

        forward(i, a)
        raw(i, b)
        fwd2(i)

        @pl.when(more)
        def _():
            project(i + 1, a)
            sum1(i + 1, a)

        relay(i, b)

        @pl.when(more)
        def _():
            sum2(i + 1, a)

        turn(i)
        fwd3(i)
        own(i, b)

        @pl.when(more)
        def _():
            sum3(i + 1, a)

        forward(i, b)
        return carry

    lax.fori_loop(0, STEPS, body, 0)

    stores = [pltpu.make_async_copy(wn, wn_o, store.at[0])]
    stores[0].start()
    for i in range(STEPS):
        await_bytes(fj.at[i, pl.ds(0, GROUP - 1)], f3r.at[i])
        stores.append(pltpu.make_async_copy(fj.at[i], fw_o.at[STEPS - 1 - i], store.at[1 + i]))
        stores.append(pltpu.make_async_copy(pb.at[i], pb_o.at[STEPS - 1 - i], store.at[1 + STEPS + i]))
    for copy in stores[1:]:
        copy.start()
    for h in range(HALVES):
        for k in range(2, 6):
            landed(STEPS - 1, h, k)
    stores.append(pltpu.make_async_copy(w.at[STEPS], bt_o, store.at[1 + 2 * STEPS]))
    stores[-1].start()

    for k in range(2):
        await_bytes((cr1, cr2)[k], cs_s.at[k])

    def left_all(i, carry):
        await_bytes(fr1.at[i], f1s.at[i])
        await_bytes(fr2.at[i, pl.ds(0, zs - 1)], f2s.at[i])
        await_bytes(fj.at[i, pl.ds(0, GROUP - 1)], f3s.at[i])
        for h in range(HALVES):
            await_bytes(rb1.at[i, h], s1s.at[i, h])
            await_bytes(rb2.at[i, h, pl.ds(0, zs - 1)], s2s.at[i, h])
            await_bytes(pj.at[i, h, pl.ds(0, GROUP - 1)], s3s.at[i, h])
            await_bytes(mr.at[i, h], mss.at[i, h])
            for k in range(6):
                await_bytes(rs_s.at[i, h, k], rss.at[i, h, k])
                await_bytes(w.at[i + 1, h, k], ags.at[i, h, k])
        return carry

    lax.fori_loop(0, STEPS, left_all, 0)
    for copy in stores:
        copy.wait()


def gradients(count, fm, wn, pb, fw, bt, beta_o, left_o, right_o):
    hb = bt.shape[2]
    batch = HALVES * hb
    both = jnp.concatenate([bt[h, 0] for h in range(HALVES)], axis=0)
    beta_o[...] = both.T
    left_o[...] = (nn(fm[...], pb[...]) / count).astype(BF16)
    right_o[...] = (nn(wn[...], fw[...]) / count).astype(BF16)


def on_device(token_ids, word_emb, state_emb, log_norm, beta_last, forward_marg, trans_left, trans_right):
    states_n = lax.axis_size("state")
    zs = states_n // GROUP
    local, hidden = state_emb.shape
    states_all = states_n * local
    vocab = word_emb.shape[0]
    ranks = trans_left.shape[1]
    batch = beta_last.shape[1]
    hb = batch // HALVES
    blk = local // BLOCKS
    padded = -(-vocab // 1024) * 1024
    if padded == vocab:
        padded += 1024
    half_ranks = ranks // 2
    dma = pltpu.SemaphoreType.DMA
    vm = pltpu.VMEM
    scratch = [
        vm((STEPS, batch), jnp.int32), vm((padded, hidden), BF16), vm((local, hidden), BF16), vm((BLOCKS, 1, blk), F32),
        vm((local, batch), BF16), vm((local, STEPS * batch), BF16), vm((local, ranks), BF16), vm((local, ranks), BF16),
        vm((STEPS, batch, hidden), BF16), vm((STEPS + 1, HALVES, BLOCKS, hb, blk), BF16),
        vm((local, STEPS * batch), BF16), vm((STEPS, HALVES, 2, hb, blk), F32), vm((HALVES, hb, ranks), F32),
        vm((HALVES, 4, hb, blk), F32), vm((16, ranks), BF16), vm((STEPS, HALVES, hb, ranks), BF16),
        vm((STEPS, HALVES, GROUP, 16, half_ranks), BF16), vm((STEPS, HALVES, GROUP - 1, 16, half_ranks), BF16),
        vm((STEPS, HALVES, zs, 16, half_ranks), BF16), vm((STEPS, HALVES, GROUP, 16, half_ranks), BF16),
        vm((STEPS, GROUP, 16, ranks), BF16), vm((STEPS, GROUP - 1, 16, ranks), BF16),
        vm((STEPS, zs, 16, ranks), BF16), vm((STEPS, GROUP, 16, ranks), BF16),
        vm((2, 8, 128), F32), vm((GROUP - 1, 8, 128), F32), vm((zs - 1, 8, 128), F32),
        vm((STEPS, HALVES, 6, hb, blk), BF16), vm((STEPS, HALVES, 6, hb, blk), BF16),
        vm((STEPS, HALVES, 8, 128), F32), vm((STEPS, HALVES, RANKS - 1, 8, 128), F32),
        dma((8,)), dma((2 + 2 * STEPS,)),
        *[dma((STEPS, HALVES)) for _ in range(6)], *[dma((STEPS,)) for _ in range(6)], dma((2,)), dma((2,)),
        *[dma((STEPS, HALVES, 6)) for _ in range(4)], *[dma((STEPS, HALVES)) for _ in range(2)],
    ]
    anywhere = pl.BlockSpec(memory_space=pl.ANY)
    wn, pb, fw, bt = pl.pallas_call(
        functools.partial(recursion, states_all, zs),
        out_shape=(
            jax.ShapeDtypeStruct((local, STEPS * batch), BF16),
            jax.ShapeDtypeStruct((STEPS, HALVES, hb, ranks), BF16),
            jax.ShapeDtypeStruct((STEPS, GROUP, 16, ranks), BF16),
            jax.ShapeDtypeStruct((HALVES, BLOCKS, hb, blk), BF16),
        ),
        in_specs=[anywhere] * 8,
        out_specs=[anywhere] * 4,
        scratch_shapes=scratch,
        compiler_params=pltpu.CompilerParams(
            collective_id=0, has_side_effects=True, vmem_limit_bytes=56 * 2**20
        ),
        name="recursion",
    )(token_ids, word_emb, state_emb, log_norm.reshape(BLOCKS, 1, blk), beta_last, forward_marg, trans_left, trans_right)
    count = STEPS * batch
    whole = lambda shape: pl.BlockSpec(shape, lambda j: (0,) * len(shape))
    return pl.pallas_call(
        functools.partial(gradients, count),
        grid=(BLOCKS,),
        out_shape=(
            jax.ShapeDtypeStruct((local, batch), BF16),
            jax.ShapeDtypeStruct((local, ranks), BF16),
            jax.ShapeDtypeStruct((local, ranks), BF16),
        ),
        in_specs=[
            pl.BlockSpec((blk, count), lambda j: (j, 0)),
            pl.BlockSpec((blk, count), lambda j: (j, 0)),
            whole((count, ranks)),
            whole((count, ranks)),
            pl.BlockSpec((HALVES, 1, hb, blk), lambda j: (0, j, 0, 0)),
        ],
        out_specs=[
            pl.BlockSpec((blk, batch), lambda j: (j, 0)),
            pl.BlockSpec((blk, ranks), lambda j: (j, 0)),
            pl.BlockSpec((blk, ranks), lambda j: (j, 0)),
        ],
        compiler_params=pltpu.CompilerParams(vmem_limit_bytes=32 * 2**20),
        name="gradients",
    )(forward_marg, wn, pb.reshape(count, ranks), fw.reshape(count, ranks), bt)


def solution(mesh):
    placed = (
        P(), P(), P("state", None), P("state"), P("state", None), P("state", None), P("state", "rank"), P("state", "rank"),
    )
    return jax.shard_map(
        on_device,
        mesh=mesh,
        in_specs=placed,
        out_specs=(P("state", None), P("state", "rank"), P("state", "rank")),
        check_vma=False,
    )
```

```python
import functools

import jax
import jax.numpy as jnp
from jax import lax
from jax.experimental import pallas as pl
from jax.experimental.pallas import tpu as pltpu
from jax.sharding import PartitionSpec as P

MESH = pl.DeviceIdType.MESH
F32 = jnp.float32
BF16 = jnp.bfloat16
GROUP = 8
RANKS = 4
BLOCKS = 2 * RANKS
HALVES = 2
STEPS = 3


def nn(a, b):
    return lax.dot_general(a, b, (((1,), (0,)), ((), ())), preferred_element_type=F32)


def nt(a, b):
    return lax.dot_general(a, b, (((1,), (1,)), ((), ())), preferred_element_type=F32)


def recursion(
    states_all, zs,
    ids, word_emb, semb, ln, beta, fm, left, right,
    left_o, right_o, bt_o,
    ids_s, ids_v, emb_v, semb_v, ln_v, beta_v, fm_v, u_v, v_v,
    tiles_v, words, w, wn, emit, acc, keep, csm, pb,
    cb, cr, xb, fs1, fr1, fr2, fj, cs, cr1, cr2,
    rs_s, rs_r, ms, mr,
    load, c1s, c1r, xs, xr, c2s, c2r, f1s, f1r, f2s, f2r, f3s, f3r, cs_s, cs_r,
    rss, rsr, ags, agr, mss, msr,
):
    state = lax.axis_index("state")
    y = lax.axis_index("rank")
    chips = zs * GROUP // 2
    g = lax.rem(state, GROUP)
    z = state // GROUP
    chip = state // 2
    core = lax.rem(state, 2)
    yp, yo, ym = lax.rem(y + 1, RANKS), lax.rem(y + 2, RANKS), lax.rem(y + 3, RANKS)
    local, ranks = left.shape
    blk = local // BLOCKS
    hb = w.shape[3]
    half = hb // 2
    batch = HALVES * hb
    hidden = semb.shape[1]
    count = STEPS * batch

    loads = [
        (ids, ids_s), (ids, ids_v), (word_emb, emb_v), (left, u_v), (semb, semb_v), (ln, ln_v), (beta, beta_v),
        (right, v_v), (fm, fm_v),
    ]
    loads = [pltpu.make_async_copy(src, dst, load.at[k]) for k, (src, dst) in enumerate(loads)]
    ids_l, idv_l, emb_l, u_l, semb_l, ln_l, beta_l, v_l, fm_l = loads
    for copy in loads[:8]:
        copy.start()

    def group_peer(d):
        p = lax.rem(g + d, GROUP)
        return p, (z * GROUP + p, y)

    def z_peer(d):
        return (lax.rem(z + d, zs) * GROUP + g, y)

    def chip_peer(d):
        return (2 * lax.rem(chip + d, chips) + core, y)

    partner = (2 * chip + 1 - core, y)
    barrier = pltpu.get_barrier_semaphore()
    greeted = [group_peer(d)[1] for d in range(1, GROUP)] + [(state, other) for other in (yp, yo, ym)]
    for dz in range(1, zs):
        for dx in range(0, GROUP, 2):
            greeted.append((lax.rem(z + dz, zs) * GROUP + lax.rem(g + dx, GROUP), y))
    for who in greeted:
        pl.semaphore_signal(barrier, inc=1, device_id=who, device_id_type=MESH)

    def send(src, dst, send_sem, recv_sem, who):
        pltpu.make_async_remote_copy(
            src_ref=src, dst_ref=dst, send_sem=send_sem, recv_sem=recv_sem, device_id=who, device_id_type=MESH
        ).start()

    def await_bytes(ref, sem):
        pltpu.make_async_copy(ref, ref, sem).wait()

    def rows(ref, j):
        return ref[pl.ds(pl.multiple_of(j * blk, blk), blk), :]

    lines = ranks // 128

    def columns1():
        def one(j, total):
            return total + nn(jnp.ones((16, blk), BF16), rows(u_v, j))

        total = lax.fori_loop(0, BLOCKS, one, jnp.zeros((16, ranks), F32))
        cs[...] = jnp.zeros_like(cs)
        for c in range(lines):
            cs[0, c:c + 1, :] = total[0:1, 128 * c:128 * c + 128]
        pl.semaphore_wait(barrier, len(greeted))
        for d in range(1, GROUP):
            send(cs.at[0], cr1.at[d - 1], cs_s.at[0], cs_r.at[0], group_peer(d)[1])

    def columns2():
        await_bytes(cr1, cs_r.at[0])
        total = cs[0]
        for d in range(GROUP - 1):
            total += cr1[d]
        cs[1] = total
        for d in range(1, zs):
            send(cs.at[1], cr2.at[d - 1], cs_s.at[1], cs_r.at[1], z_peer(d))

    def columns3():
        await_bytes(cr2, cs_r.at[1])
        total = cs[1]
        for d in range(zs - 1):
            total += cr2[d]
        line = jnp.concatenate([total[c:c + 1] for c in range(lines)], axis=1)
        high = line.astype(BF16)
        rest = line - high.astype(F32)
        mid = rest.astype(BF16)
        low = (rest - mid.astype(F32)).astype(BF16)
        parts = [x.astype(F32) for x in (high, mid, low)] + [jnp.zeros((13, ranks), F32)]
        csm[...] = jnp.concatenate(parts, axis=0).astype(BF16)

    def find_words(t):
        def one(k, carry):
            tiles_v[k] = emb_v[lax.shift_right_logical(ids_s[t, k], 4)]
            return carry

        lax.fori_loop(0, batch, one, 0, unroll=8)
        lane = lax.broadcasted_iota(jnp.int32, (batch, 16 * batch), 1).astype(F32)
        pick = jnp.where(lane == place[:, t:t + 1], 1.0, 0.0).astype(BF16)
        words[t] = nn(pick, tiles_v[...].reshape(16 * batch, hidden)).astype(BF16)

    ids_l.wait()
    idv_l.wait()
    inside = jnp.bitwise_and(ids_v[...], 15) + 16 * lax.broadcasted_iota(jnp.int32, (STEPS, batch), 1)
    place = jnp.concatenate([inside.astype(F32), jnp.zeros((8 - STEPS, batch), F32)], axis=0).T
    emb_l.wait()
    find_words(STEPS - 1)
    u_l.wait()
    columns1()

    semb_l.wait()
    ln_l.wait()
    beta_l.wait()
    v_l.wait()
    fm_l.start()
    eye = jnp.where(
        lax.broadcasted_iota(jnp.int32, (batch, batch), 0) == lax.broadcasted_iota(jnp.int32, (batch, batch), 1), 1.0, 0.0
    ).astype(BF16)

    def first(j, total):
        logits = nt(words[STEPS - 1], rows(semb_v, j))
        em = jnp.exp(logits - ln_v[j])
        wt = (em * nt(eye, rows(beta_v, j))).astype(BF16)
        for h in range(HALVES):
            w[0, h, j] = wt[h * hb:(h + 1) * hb]
        return total + nn(wt, rows(v_v, j))

    total = lax.fori_loop(0, BLOCKS, first, jnp.zeros((batch, ranks), F32))
    for h in range(HALVES):
        acc[h] = total[h * hb:(h + 1) * hb]

    def sum1(i, h):
        cb[i, h] = acc[h, pl.ds(pl.multiple_of(half * (1 - core), half), half), :].astype(BF16)
        send(cb.at[i, h], cr.at[i, h], c1s.at[i, h], c1r.at[i, h], partner)

    def sum2(i, h):
        await_bytes(cr.at[i, h], c1r.at[i, h])
        mine = acc[h, pl.ds(pl.multiple_of(half * core, half), half), :]
        xb[i, h, chip] = (mine + cr[i, h].astype(F32)).astype(BF16)
        for d in range(1, chips):
            send(xb.at[i, h, chip], xb.at[i, h, chip], xs.at[i, h], xr.at[i, h], chip_peer(d))

    def sum3(i, h):
        await_bytes(xb.at[i, h, pl.ds(0, chips - 1)], xr.at[i, h])
        total = xb[i, h, 0].astype(F32)
        for d in range(1, chips):
            total += xb[i, h, d].astype(F32)
        pb[STEPS - 1 - i, h, core] = total.astype(BF16)
        place_of = pb.at[STEPS - 1 - i, h, core]
        send(place_of, place_of, c2s.at[i, h], c2r.at[i, h], partner)

    def fwd1(i):
        t = STEPS - 1 - i

        def one(j, total):
            cols = fm_v[pl.ds(pl.multiple_of(j * blk, blk), blk), pl.ds(pl.multiple_of(t * batch, batch), batch)]
            return total + nn(cols.T, rows(u_v, j))

        total = lax.fori_loop(0, BLOCKS, one, jnp.zeros((batch, ranks), F32))
        for p in range(GROUP):
            fs1[i, p] = total[16 * p:16 * p + 16].astype(BF16)
        for d in range(1, GROUP):
            p, who = group_peer(d)
            send(fs1.at[i, p], fr1.at[i, d - 1], f1s.at[i], f1r.at[i], who)

    def fwd2(i):
        await_bytes(fr1.at[i], f1r.at[i])
        total = fs1[i, g].astype(F32)
        for d in range(GROUP - 1):
            total += fr1[i, d].astype(F32)
        fr2[i, z] = total.astype(BF16)
        for d in range(1, zs):
            send(fr2.at[i, z], fr2.at[i, z], f2s.at[i], f2r.at[i], z_peer(d))

    def fwd3(i):
        t = STEPS - 1 - i
        await_bytes(fr2.at[i, pl.ds(0, zs - 1)], f2r.at[i])
        total = fr2[i, 0].astype(F32)
        for d in range(1, zs):
            total += fr2[i, d].astype(F32)
        fj[t, g] = (total / states_all).astype(BF16)
        for d in range(1, GROUP):
            send(fj.at[t, g], fj.at[t, g], f3s.at[i], f3r.at[i], group_peer(d)[1])

    def raw(i, h):
        await_bytes(pb.at[STEPS - 1 - i, h, 0], c2r.at[i, h])
        proj = pb[STEPS - 1 - i, h].reshape(hb, ranks)
        sums = nt(csm[...], proj)
        ms[i, h, 0:1, 0:hb] = sums[0:1] + sums[1:2] + sums[2:3]
        for d, who in enumerate((yp, yo, ym)):
            send(ms.at[i, h], mr.at[i, h, d], mss.at[i, h], msr.at[i, h], (state, who))
        for part in range(2):
            for d, who in ((1, yo), (0, yp), (2, ym)):
                rs_s[i, h, part, d] = nt(proj, rows(u_v, 2 * who + part)).astype(BF16)
                send(rs_s.at[i, h, part, d], rs_r.at[i, h, part, d], rss.at[i, h, part], rsr.at[i, h, part], (state, who))
        for part in range(2):
            keep[h, part] = nt(proj, rows(u_v, 2 * y + part))

    def mass_of(i, h):
        await_bytes(mr.at[i, h], msr.at[i, h])
        mass = ms[i, h] + mr[i, h, 0] + mr[i, h, 1] + mr[i, h, 2]
        return mass.T[0:hb, 0:1] / states_all

    def own(i, h):
        mass = mass_of(i, h)
        for part in range(2):
            await_bytes(rs_r.at[i, h, part], rsr.at[i, h, part])
            total = keep[h, part]
            for d in range(RANKS - 1):
                total += rs_r[i, h, part, d].astype(F32)
            new = (total / mass).astype(BF16).astype(F32)
            j = 2 * y + part
            w[i + 1, h, j] = (emit[i, h, part] * new).astype(BF16)
            for who in (yo, yp, ym):
                send(w.at[i + 1, h, j], w.at[i + 1, h, j], ags.at[i, h, part], agr.at[i, h, part], (state, who))

    def landed(i, h, part):
        await_bytes(w.at[i + 1, h, pl.ds(0, RANKS - 1)], agr.at[i, h, part])

    def project(i, h):
        def term(j):
            return nn(w[i, h, j], rows(v_v, j))

        total = term(2 * y) + term(2 * y + 1)
        for part in range(2):
            landed(i - 1, h, part)
            for who in (yp, yo, ym):
                total += term(2 * who + part)
        acc[h] = total
        sum1(i, h)

    def turn(i):
        t = STEPS - 1 - i

        def one(j, carry):
            both = jnp.concatenate([w[i, h, j] for h in range(HALVES)], axis=0)
            wn[pl.ds(pl.multiple_of(j * blk, blk), blk), pl.ds(pl.multiple_of(t * batch, batch), batch)] = both.T
            return carry

        lax.fori_loop(0, BLOCKS, one, 0)

    def gradients():
        for i in range(STEPS):
            await_bytes(fj.at[i, pl.ds(0, GROUP - 1)], f3r.at[i])
        proj = pb[...].reshape(count, ranks)
        fwd = fj[...].reshape(count, ranks)

        def one(j, carry):
            at = pl.ds(pl.multiple_of(j * blk, blk), blk)
            left_o[at, :] = (nn(fm_v[at, :], proj) / count).astype(BF16)
            right_o[at, :] = (nn(wn[at, :], fwd) / count).astype(BF16)
            return carry

        lax.fori_loop(0, BLOCKS, one, 0)

    a, b = 0, 1
    sum1(0, a)
    sum1(0, b)
    columns2()
    sum2(0, a)

    ms[...] = jnp.zeros_like(ms)
    for t in range(STEPS - 1):
        find_words(t)
    for i in range(STEPS - 1):
        for part in range(2):
            logits = nt(words[STEPS - 2 - i], rows(semb_v, 2 * y + part))
            em = jnp.exp(logits - ln_v[2 * y + part])
            for h in range(HALVES):
                emit[i, h, part] = em[h * hb:(h + 1) * hb]
    emit[STEPS - 1] = jnp.ones_like(emit[STEPS - 1])
    columns3()
    fm_l.wait()
    fwd1(0)
    sum2(0, b)
    sum3(0, a)

    def body(i, carry):
        more = i < STEPS - 1
        raw(i, a)

        @pl.when(i > 0)
        def _():
            sum2(i, b)

        fwd2(i)
        turn(i)

        @pl.when(more)
        def _():
            fwd1(i + 1)

        own(i, a)
        sum3(i, b)
        raw(i, b)
        fwd3(i)

        @pl.when(more)
        def _():
            project(i + 1, a)
            sum2(i + 1, a)

        @pl.when(i == STEPS - 1)
        def _():
            gradients()

        own(i, b)

        @pl.when(more)
        def _():
            project(i + 1, b)
            sum3(i + 1, a)

        return carry

    lax.fori_loop(0, STEPS, body, 0)

    for h in range(HALVES):
        for part in range(2):
            landed(STEPS - 1, h, part)
    bt_o[...] = w[STEPS]

    for k in range(2):
        await_bytes((cr1, cr2)[k], cs_s.at[k])

    def left_all(i, carry):
        await_bytes(fr1.at[i], f1s.at[i])
        await_bytes(fr2.at[i, pl.ds(0, zs - 1)], f2s.at[i])
        await_bytes(fj.at[i, pl.ds(0, GROUP - 1)], f3s.at[i])
        for h in range(HALVES):
            await_bytes(cr.at[i, h], c1s.at[i, h])
            await_bytes(xb.at[i, h, pl.ds(0, chips - 1)], xs.at[i, h])
            await_bytes(pb.at[i, h, 0], c2s.at[i, h])
            await_bytes(mr.at[i, h], mss.at[i, h])
            for part in range(2):
                await_bytes(rs_r.at[i, h, part], rss.at[i, h, part])
                await_bytes(w.at[i + 1, h, pl.ds(0, RANKS - 1)], ags.at[i, h, part])
        return carry

    lax.fori_loop(0, STEPS, left_all, 0)


def finish(bt, left, right, beta_o, left_o, right_o, beta_v, sems):
    copies = [pltpu.make_async_copy(left, left_o, sems.at[0]), pltpu.make_async_copy(right, right_o, sems.at[1])]
    for copy in copies:
        copy.start()
    blk = bt.shape[3]

    def one(j, carry):
        both = jnp.concatenate([bt[h, j] for h in range(HALVES)], axis=0)
        beta_v[pl.ds(pl.multiple_of(j * blk, blk), blk), :] = both.T
        return carry

    lax.fori_loop(0, BLOCKS, one, 0)
    copies.append(pltpu.make_async_copy(beta_v, beta_o, sems.at[2]))
    copies[2].start()
    for copy in copies:
        copy.wait()


def on_device(token_ids, word_emb, state_emb, log_norm, beta_last, forward_marg, trans_left, trans_right):
    states_n = lax.axis_size("state")
    zs = states_n // GROUP
    chips = states_n // 2
    local, hidden = state_emb.shape
    states_all = states_n * local
    vocab = word_emb.shape[0]
    ranks = trans_left.shape[1]
    batch = beta_last.shape[1]
    hb = batch // HALVES
    blk = local // BLOCKS
    dma = pltpu.SemaphoreType.DMA
    vm = pltpu.VMEM
    scratch = [
        pltpu.SMEM((STEPS, batch), jnp.int32), vm((STEPS, batch), jnp.int32), vm((vocab // 16, 16, hidden), BF16),
        vm((local, hidden), BF16), vm((BLOCKS, 1, blk), F32), vm((local, batch), BF16), vm((local, STEPS * batch), BF16),
        vm((local, ranks), BF16), vm((local, ranks), BF16),
        vm((batch, 16, hidden), BF16), vm((STEPS, batch, hidden), BF16), vm((STEPS + 1, HALVES, BLOCKS, hb, blk), BF16),
        vm((local, STEPS * batch), BF16), vm((STEPS, HALVES, 2, hb, blk), F32), vm((HALVES, hb, ranks), F32),
        vm((HALVES, 2, hb, blk), F32), vm((16, ranks), BF16), vm((STEPS, HALVES, 2, hb // 2, ranks), BF16),
        vm((STEPS, HALVES, hb // 2, ranks), BF16), vm((STEPS, HALVES, hb // 2, ranks), BF16),
        vm((STEPS, HALVES, chips, hb // 2, ranks), BF16),
        vm((STEPS, GROUP, 16, ranks), BF16), vm((STEPS, GROUP - 1, 16, ranks), BF16),
        vm((STEPS, zs, 16, ranks), BF16), vm((STEPS, GROUP, 16, ranks), BF16),
        vm((2, 8, 128), F32), vm((GROUP - 1, 8, 128), F32), vm((zs - 1, 8, 128), F32),
        vm((STEPS, HALVES, 2, RANKS - 1, hb, blk), BF16), vm((STEPS, HALVES, 2, RANKS - 1, hb, blk), BF16),
        vm((STEPS, HALVES, 8, 128), F32), vm((STEPS, HALVES, RANKS - 1, 8, 128), F32),
        dma((9,)),
        *[dma((STEPS, HALVES)) for _ in range(6)], *[dma((STEPS,)) for _ in range(6)], dma((2,)), dma((2,)),
        *[dma((STEPS, HALVES, 2)) for _ in range(4)], *[dma((STEPS, HALVES)) for _ in range(2)],
    ]
    anywhere = pl.BlockSpec(memory_space=pl.ANY)
    inside = pl.BlockSpec(memory_space=pltpu.VMEM)
    left, right, bt = pl.pallas_call(
        functools.partial(recursion, states_all, zs),
        out_shape=(vm((local, ranks), BF16), vm((local, ranks), BF16), vm((HALVES, BLOCKS, hb, blk), BF16)),
        in_specs=[anywhere] * 8,
        out_specs=[inside] * 3,
        scratch_shapes=scratch,
        compiler_params=pltpu.CompilerParams(
            collective_id=0, has_side_effects=True, vmem_limit_bytes=46 * 2**20
        ),
        name="recursion",
    )(
        token_ids, word_emb.reshape(vocab // 16, 16, hidden), state_emb, log_norm.reshape(BLOCKS, 1, blk), beta_last,
        forward_marg, trans_left, trans_right,
    )
    beta, left, right = pl.pallas_call(
        finish,
        out_shape=(
            jax.ShapeDtypeStruct((local, batch), BF16),
            jax.ShapeDtypeStruct((local, ranks), BF16),
            jax.ShapeDtypeStruct((local, ranks), BF16),
        ),
        in_specs=[inside] * 3,
        out_specs=[anywhere] * 3,
        scratch_shapes=[vm((local, batch), BF16), dma((3,))],
        compiler_params=pltpu.CompilerParams(vmem_limit_bytes=16 * 2**20),
        name="finish",
    )(bt, left, right)
    return beta, left, right


def solution(mesh):
    placed = (
        P(), P(), P("state", None), P("state"), P("state", None), P("state", None), P("state", "rank"), P("state", "rank"),
    )
    return jax.shard_map(
        on_device,
        mesh=mesh,
        in_specs=placed,
        out_specs=(P("state", None), P("state", "rank"), P("state", "rank")),
        check_vma=False,
    )
```

```python
import functools

import jax
import jax.numpy as jnp
from jax import lax
from jax.experimental import pallas as pl
from jax.experimental.pallas import tpu as pltpu
from jax.sharding import PartitionSpec as P

MESH = pl.DeviceIdType.MESH
F32 = jnp.float32
BF16 = jnp.bfloat16
GROUP = 8
RANKS = 4
BLOCKS = 2 * RANKS
CHAINS = 4
STEPS = 3


def nn(a, b):
    return lax.dot_general(a, b, (((1,), (0,)), ((), ())), preferred_element_type=F32)


def nt(a, b):
    return lax.dot_general(a, b, (((1,), (1,)), ((), ())), preferred_element_type=F32)


def recursion(
    states_all, zs,
    ids, word_emb, semb, ln, beta, fm, left, right,
    left_o, right_o, bt_o,
    ids_s, ids_v, emb_v, semb_v, ln_v, beta_v, fm_v, u_v, v_v,
    tiles_v, words, w, wn, emit, acc, keep, csm, pb,
    cb, cr, xb, facc, fs1, fr1, fr2, fj, cs, cr1, cr2,
    rs_s, rs_r, ms, mr,
    load, c1s, c1r, xs, xr, c2s, c2r, f1s, f1r, f2s, f2r, f3s, f3r, cs_s, cs_r,
    rss, rsr, ags, agr, mss, msr,
):
    state = lax.axis_index("state")
    y = lax.axis_index("rank")
    chips = zs * GROUP // 2
    g = lax.rem(state, GROUP)
    z = state // GROUP
    chip = state // 2
    core = lax.rem(state, 2)
    yp, yo, ym = lax.rem(y + 1, RANKS), lax.rem(y + 2, RANKS), lax.rem(y + 3, RANKS)
    local, ranks = left.shape
    blk = local // BLOCKS
    hb = w.shape[3]
    half = hb // 2
    batch = CHAINS * hb
    hidden = semb.shape[1]
    count = STEPS * batch

    loads = [
        (ids, ids_s), (ids, ids_v), (word_emb, emb_v), (semb, semb_v), (ln, ln_v), (beta, beta_v), (left, u_v), (fm, fm_v),
    ]
    loads = [pltpu.make_async_copy(src, dst, load.at[k]) for k, (src, dst) in enumerate(loads)]
    ids_l, idv_l, emb_l, semb_l, ln_l, beta_l, u_l, fm_l = loads

    def v_l(j):
        at = pl.ds(pl.multiple_of(j * blk, blk), blk)
        return pltpu.make_async_copy(right.at[at], v_v.at[at], load.at[8 + j])

    for copy in loads[:6] + [v_l(j) for j in range(BLOCKS)] + loads[6:]:
        copy.start()

    def group_peer(d):
        p = lax.rem(g + d, GROUP)
        return p, (z * GROUP + p, y)

    def z_peer(d):
        return (lax.rem(z + d, zs) * GROUP + g, y)

    def chip_peer(d):
        return (2 * lax.rem(chip + d, chips) + core, y)

    partner = (2 * chip + 1 - core, y)
    barrier = pltpu.get_barrier_semaphore()
    greeted = [group_peer(d)[1] for d in range(1, GROUP)] + [(state, other) for other in (yp, yo, ym)]
    for dz in range(1, zs):
        for dx in range(0, GROUP, 2):
            greeted.append((lax.rem(z + dz, zs) * GROUP + lax.rem(g + dx, GROUP), y))
    for who in greeted:
        pl.semaphore_signal(barrier, inc=1, device_id=who, device_id_type=MESH)

    def send(src, dst, send_sem, recv_sem, who):
        pltpu.make_async_remote_copy(
            src_ref=src, dst_ref=dst, send_sem=send_sem, recv_sem=recv_sem, device_id=who, device_id_type=MESH
        ).start()

    def await_bytes(ref, sem):
        pltpu.make_async_copy(ref, ref, sem).wait()

    def each(first, last, act):
        def one(d, carry):
            act(d)
            return carry

        lax.fori_loop(first, last, one, 0, unroll=True)

    def rows(ref, j):
        return ref[pl.ds(pl.multiple_of(j * blk, blk), blk), :]

    lines = ranks // 128

    def columns1():
        def one(j, total):
            return total + nn(jnp.ones((16, blk), BF16), rows(u_v, j))

        total = lax.fori_loop(0, BLOCKS, one, jnp.zeros((16, ranks), F32))
        cs[...] = jnp.zeros_like(cs)
        for c in range(lines):
            cs[0, c:c + 1, :] = total[0:1, 128 * c:128 * c + 128]
        for d in range(1, GROUP):
            send(cs.at[0], cr1.at[d - 1], cs_s.at[0], cs_r.at[0], group_peer(d)[1])

    def columns2():
        await_bytes(cr1, cs_r.at[0])
        total = cs[0]
        for d in range(GROUP - 1):
            total += cr1[d]
        cs[1] = total
        for d in range(1, zs):
            send(cs.at[1], cr2.at[d - 1], cs_s.at[1], cs_r.at[1], z_peer(d))

    def columns3():
        await_bytes(cr2, cs_r.at[1])
        total = cs[1]
        for d in range(zs - 1):
            total += cr2[d]
        line = jnp.concatenate([total[c:c + 1] for c in range(lines)], axis=1)
        high = line.astype(BF16)
        rest = line - high.astype(F32)
        mid = rest.astype(BF16)
        low = (rest - mid.astype(F32)).astype(BF16)
        parts = [x.astype(F32) for x in (high, mid, low)] + [jnp.zeros((13, ranks), F32)]
        csm[...] = jnp.concatenate(parts, axis=0).astype(BF16)

    def find_words(t):
        def one(k, carry):
            tiles_v[k] = emb_v[lax.shift_right_logical(ids_s[t, k], 4)]
            return carry

        lax.fori_loop(0, batch, one, 0, unroll=8)
        lane = lax.broadcasted_iota(jnp.int32, (batch, 16 * batch), 1).astype(F32)
        pick = jnp.where(lane == place[:, t:t + 1], 1.0, 0.0).astype(BF16)
        words[t] = nn(pick, tiles_v[...].reshape(16 * batch, hidden)).astype(BF16)

    ids_l.wait()
    idv_l.wait()
    inside = jnp.bitwise_and(ids_v[...], 15) + 16 * lax.broadcasted_iota(jnp.int32, (STEPS, batch), 1)
    place = jnp.concatenate([inside.astype(F32), jnp.zeros((8 - STEPS, batch), F32)], axis=0).T
    emb_l.wait()
    find_words(STEPS - 1)

    semb_l.wait()
    ln_l.wait()
    beta_l.wait()
    eye = jnp.where(
        lax.broadcasted_iota(jnp.int32, (batch, batch), 0) == lax.broadcasted_iota(jnp.int32, (batch, batch), 1), 1.0, 0.0
    ).astype(BF16)

    def first(j, total):
        logits = nt(words[STEPS - 1], rows(semb_v, j))
        em = jnp.exp(logits - ln_v[j])
        wt = (em * nt(eye, rows(beta_v, j))).astype(BF16)
        for h in range(CHAINS):
            w[0, h, j] = wt[h * hb:(h + 1) * hb]
        v_l(j).wait()
        return total + nn(wt, rows(v_v, j))

    total = lax.fori_loop(0, BLOCKS, first, jnp.zeros((batch, ranks), F32), unroll=2)
    for h in range(CHAINS):
        acc[h] = total[h * hb:(h + 1) * hb]

    pl.semaphore_wait(barrier, len(greeted))

    def sum1(i, h):
        cb[i, h] = acc[h, pl.ds(pl.multiple_of(half * (1 - core), half), half), :].astype(BF16)
        send(cb.at[i, h], cr.at[i, h], c1s.at[i, h], c1r.at[i, h], partner)

    def sum2(i, h):
        await_bytes(cr.at[i, h], c1r.at[i, h])
        mine = acc[h, pl.ds(pl.multiple_of(half * core, half), half), :]
        xb[i, h, chip] = (mine + cr[i, h].astype(F32)).astype(BF16)
        mine = xb.at[i, h, chip]
        each(1, chips, lambda d: send(mine, mine, xs.at[i, h], xr.at[i, h], chip_peer(d)))

    def sum3(i, h):
        await_bytes(xb.at[i, h, pl.ds(0, chips - 1)], xr.at[i, h])
        total = xb[i, h, 0].astype(F32)
        for d in range(1, chips):
            total += xb[i, h, d].astype(F32)
        pb[STEPS - 1 - i, h, core] = total.astype(BF16)
        place_of = pb.at[STEPS - 1 - i, h, core]
        send(place_of, place_of, c2s.at[i, h], c2r.at[i, h], partner)

    def fwd1(i, part):
        t = STEPS - 1 - i

        def one(j, total):
            cols = fm_v[pl.ds(pl.multiple_of(j * blk, blk), blk), pl.ds(pl.multiple_of(t * batch, batch), batch)]
            return total + nn(cols.T, rows(u_v, j))

        @pl.when(part == 0)
        def _():
            facc[...] = jnp.zeros_like(facc)

        count = BLOCKS // CHAINS
        total = facc[...]
        for j in range(count):
            total = one(part * count + j, total)
        facc[...] = total

        @pl.when(part == CHAINS - 1)
        def _():
            for p in range(GROUP):
                fs1[i, p] = facc[16 * p:16 * p + 16].astype(BF16)

            def out(d):
                p, who = group_peer(d)
                send(fs1.at[i, p], fr1.at[i, d - 1], f1s.at[i], f1r.at[i], who)

            each(1, GROUP, out)

    def fwd2(i):
        await_bytes(fr1.at[i], f1r.at[i])
        total = fs1[i, g].astype(F32)
        for d in range(GROUP - 1):
            total += fr1[i, d].astype(F32)
        fr2[i, z] = total.astype(BF16)
        for d in range(1, zs):
            send(fr2.at[i, z], fr2.at[i, z], f2s.at[i], f2r.at[i], z_peer(d))

    def fwd3(i):
        t = STEPS - 1 - i
        await_bytes(fr2.at[i, pl.ds(0, zs - 1)], f2r.at[i])
        total = fr2[i, 0].astype(F32)
        for d in range(1, zs):
            total += fr2[i, d].astype(F32)
        fj[t, g] = (total / states_all).astype(BF16)
        each(1, GROUP, lambda d: send(fj.at[t, g], fj.at[t, g], f3s.at[i], f3r.at[i], group_peer(d)[1]))

    def raw(i, h):
        await_bytes(pb.at[STEPS - 1 - i, h, 0], c2r.at[i, h])
        proj = pb[STEPS - 1 - i, h].reshape(hb, ranks)

        def to_owner(d):
            who = lax.rem(y + 1 + d, RANKS)
            for part in range(2):
                rs_s[i, h, d, part] = nt(proj, rows(u_v, 2 * who + part)).astype(BF16)
            send(rs_s.at[i, h, d], rs_r.at[i, h, d], rss.at[i, h], rsr.at[i, h], (state, who))

        each(0, RANKS - 1, to_owner)
        pl.when(jnp.logical_and(i == 0, h == 0))(columns3)
        sums = nt(csm[...], proj)
        ms[i, h, 0:1, 0:hb] = sums[0:1] + sums[1:2] + sums[2:3]
        for d, who in enumerate((yp, yo, ym)):
            send(ms.at[i, h], mr.at[i, h, d], mss.at[i, h], msr.at[i, h], (state, who))

    def raw_own(i, h):
        proj = pb[STEPS - 1 - i, h].reshape(hb, ranks)
        for part in range(2):
            keep[h, part] = nt(proj, rows(u_v, 2 * y + part))

    def mass_of(i, h):
        await_bytes(mr.at[i, h], msr.at[i, h])
        mass = ms[i, h] + mr[i, h, 0] + mr[i, h, 1] + mr[i, h, 2]
        return mass.T[0:hb, 0:1] / states_all

    def own(i, h):
        await_bytes(rs_r.at[i, h], rsr.at[i, h])
        mass = mass_of(i, h)
        for part in range(2):
            total = keep[h, part]
            for d in range(RANKS - 1):
                total += rs_r[i, h, d, part].astype(F32)
            new = (total / mass).astype(BF16).astype(F32)
            w[i + 1, h, 2 * y + part] = (emit[i, h, part] * new).astype(BF16)
        shard = w.at[i + 1, h, pl.ds(2 * y, 2)]
        for who in (yo, yp, ym):
            send(shard, shard, ags.at[i, h], agr.at[i, h], (state, who))

    def landed(i, h):
        await_bytes(w.at[i + 1, h, pl.ds(0, 2 * (RANKS - 1))], agr.at[i, h])

    def project(i, h):
        def term(j):
            return nn(w[i, h, j], rows(v_v, j))

        def shard(who):
            return term(2 * who) + term(2 * who + 1)

        total = shard(y)
        landed(i - 1, h)
        acc[h] = total + shard(yp) + shard(yo) + shard(ym)
        sum1(i, h)

    def turn(i):
        t = STEPS - 1 - i

        def one(j, carry):
            both = jnp.concatenate([w[i, h, j] for h in range(CHAINS)], axis=0)
            wn[pl.ds(pl.multiple_of(j * blk, blk), blk), pl.ds(pl.multiple_of(t * batch, batch), batch)] = both.T
            return carry

        lax.fori_loop(0, BLOCKS, one, 0)

    def grad_left():
        proj = pb[...].reshape(count, ranks)

        def one(j, carry):
            at = pl.ds(pl.multiple_of(j * blk, blk), blk)
            left_o[at, :] = (nn(fm_v[at, :], proj) / count).astype(BF16)
            return carry

        lax.fori_loop(0, BLOCKS, one, 0)

    def grad_right():
        for i in range(STEPS):
            await_bytes(fj.at[i, pl.ds(0, GROUP - 1)], f3r.at[i])
        fwd = fj[...].reshape(count, ranks)

        def one(j, carry):
            at = pl.ds(pl.multiple_of(j * blk, blk), blk)
            right_o[at, :] = (nn(wn[at, :], fwd) / count).astype(BF16)
            return carry

        lax.fori_loop(0, BLOCKS, one, 0)

    each(0, CHAINS, lambda h: sum1(0, h))
    u_l.wait()
    columns1()
    sum2(0, 0)

    ms[...] = jnp.zeros_like(ms)
    for t in range(STEPS - 1):
        find_words(t)
    for i in range(STEPS - 1):
        for part in range(2):
            logits = nt(words[STEPS - 2 - i], rows(semb_v, 2 * y + part))
            em = jnp.exp(logits - ln_v[2 * y + part])
            for h in range(CHAINS):
                emit[i, h, part] = em[h * hb:(h + 1) * hb]
    emit[STEPS - 1] = jnp.ones_like(emit[STEPS - 1])
    columns2()
    sum2(0, 1)
    fm_l.wait()
    lax.fori_loop(0, CHAINS, lambda k, carry: (fwd1(0, k), carry)[1], 0)
    sum3(0, 0)

    def turn_of(n, carry):
        i, k = n // CHAINS, n % CHAINS
        raw(i, k)

        @pl.when(n >= 1)
        def _():
            own((n - 1) // CHAINS, (n - 1) % CHAINS)

        i2, k2 = (n + 2) // CHAINS, (n + 2) % CHAINS
        more = i2 < STEPS

        @pl.when(jnp.logical_and(n >= 2, more))
        def _():
            project(i2, k2)

        pl.when(i < STEPS - 1)(lambda: fwd1(i + 1, k))
        pl.when(more)(lambda: sum2(i2, k2))
        pl.when(k == 0)(lambda: fwd2(i))
        pl.when(k == 1)(lambda: fwd3(i))
        pl.when(k == 2)(lambda: turn(i))
        pl.when(n == CHAINS * STEPS - 1)(grad_right)
        i3, k3 = (n + 1) // CHAINS, (n + 1) % CHAINS
        pl.when(i3 < STEPS)(lambda: sum3(i3, k3))
        raw_own(i, k)
        return carry

    lax.fori_loop(0, CHAINS * STEPS, turn_of, 0)
    own(STEPS - 1, CHAINS - 1)
    grad_left()

    each(0, CHAINS, lambda h: landed(STEPS - 1, h))
    bt_o[...] = w[STEPS]

    for k in range(2):
        await_bytes((cr1, cr2)[k], cs_s.at[k])

    def left_all(i, carry):
        await_bytes(fr1.at[i], f1s.at[i])
        await_bytes(fr2.at[i, pl.ds(0, zs - 1)], f2s.at[i])
        await_bytes(fj.at[i, pl.ds(0, GROUP - 1)], f3s.at[i])
        def chain(h):
            await_bytes(cr.at[i, h], c1s.at[i, h])
            await_bytes(xb.at[i, h, pl.ds(0, chips - 1)], xs.at[i, h])
            await_bytes(pb.at[i, h, 0], c2s.at[i, h])
            await_bytes(mr.at[i, h], mss.at[i, h])
            await_bytes(rs_r.at[i, h], rss.at[i, h])
            await_bytes(w.at[i + 1, h, pl.ds(0, 2 * (RANKS - 1))], ags.at[i, h])

        each(0, CHAINS, chain)
        return carry

    lax.fori_loop(0, STEPS, left_all, 0)


def finish(bt, left, right, beta_o, left_o, right_o, beta_v, sems):
    copies = [pltpu.make_async_copy(left, left_o, sems.at[0]), pltpu.make_async_copy(right, right_o, sems.at[1])]
    for copy in copies:
        copy.start()
    blk = bt.shape[3]

    def one(j, carry):
        both = jnp.concatenate([bt[h, j] for h in range(CHAINS)], axis=0)
        beta_v[pl.ds(pl.multiple_of(j * blk, blk), blk), :] = both.T
        return carry

    lax.fori_loop(0, BLOCKS, one, 0)
    copies.append(pltpu.make_async_copy(beta_v, beta_o, sems.at[2]))
    copies[2].start()
    for copy in copies:
        copy.wait()


def on_device(token_ids, word_emb, state_emb, log_norm, beta_last, forward_marg, trans_left, trans_right):
    states_n = lax.axis_size("state")
    zs = states_n // GROUP
    chips = states_n // 2
    local, hidden = state_emb.shape
    states_all = states_n * local
    vocab = word_emb.shape[0]
    ranks = trans_left.shape[1]
    batch = beta_last.shape[1]
    hb = batch // CHAINS
    blk = local // BLOCKS
    dma = pltpu.SemaphoreType.DMA
    vm = pltpu.VMEM
    scratch = [
        pltpu.SMEM((STEPS, batch), jnp.int32), vm((STEPS, batch), jnp.int32), vm((vocab // 16, 16, hidden), BF16),
        vm((local, hidden), BF16), vm((BLOCKS, 1, blk), F32), vm((local, batch), BF16), vm((local, STEPS * batch), BF16),
        vm((local, ranks), BF16), vm((local, ranks), BF16),
        vm((batch, 16, hidden), BF16), vm((STEPS, batch, hidden), BF16), vm((STEPS + 1, CHAINS, BLOCKS, hb, blk), BF16),
        vm((local, STEPS * batch), BF16), vm((STEPS, CHAINS, 2, hb, blk), F32), vm((CHAINS, hb, ranks), F32),
        vm((CHAINS, 2, hb, blk), F32), vm((16, ranks), BF16), vm((STEPS, CHAINS, 2, hb // 2, ranks), BF16),
        vm((STEPS, CHAINS, hb // 2, ranks), BF16), vm((STEPS, CHAINS, hb // 2, ranks), BF16),
        vm((STEPS, CHAINS, chips, hb // 2, ranks), BF16),
        vm((batch, ranks), F32),
        vm((STEPS, GROUP, 16, ranks), BF16), vm((STEPS, GROUP - 1, 16, ranks), BF16),
        vm((STEPS, zs, 16, ranks), BF16), vm((STEPS, GROUP, 16, ranks), BF16),
        vm((2, 8, 128), F32), vm((GROUP - 1, 8, 128), F32), vm((zs - 1, 8, 128), F32),
        vm((STEPS, CHAINS, RANKS - 1, 2, hb, blk), BF16), vm((STEPS, CHAINS, RANKS - 1, 2, hb, blk), BF16),
        vm((STEPS, CHAINS, 8, 128), F32), vm((STEPS, CHAINS, RANKS - 1, 8, 128), F32),
        dma((8 + BLOCKS,)),
        *[dma((STEPS, CHAINS)) for _ in range(6)], *[dma((STEPS,)) for _ in range(6)], dma((2,)), dma((2,)),
        *[dma((STEPS, CHAINS)) for _ in range(6)],
    ]
    anywhere = pl.BlockSpec(memory_space=pl.ANY)
    inside = pl.BlockSpec(memory_space=pltpu.VMEM)
    left, right, bt = pl.pallas_call(
        functools.partial(recursion, states_all, zs),
        out_shape=(vm((local, ranks), BF16), vm((local, ranks), BF16), vm((CHAINS, BLOCKS, hb, blk), BF16)),
        in_specs=[anywhere] * 8,
        out_specs=[inside] * 3,
        scratch_shapes=scratch,
        compiler_params=pltpu.CompilerParams(
            collective_id=0, has_side_effects=True, vmem_limit_bytes=46 * 2**20
        ),
        name="recursion",
    )(
        token_ids, word_emb.reshape(vocab // 16, 16, hidden), state_emb, log_norm.reshape(BLOCKS, 1, blk), beta_last,
        forward_marg, trans_left, trans_right,
    )
    beta, left, right = pl.pallas_call(
        finish,
        out_shape=(
            jax.ShapeDtypeStruct((local, batch), BF16),
            jax.ShapeDtypeStruct((local, ranks), BF16),
            jax.ShapeDtypeStruct((local, ranks), BF16),
        ),
        in_specs=[inside] * 3,
        out_specs=[anywhere] * 3,
        scratch_shapes=[vm((local, batch), BF16), dma((3,))],
        compiler_params=pltpu.CompilerParams(vmem_limit_bytes=16 * 2**20),
        name="finish",
    )(bt, left, right)
    return beta, left, right


def solution(mesh):
    placed = (
        P(), P(), P("state", None), P("state"), P("state", None), P("state", None), P("state", "rank"), P("state", "rank"),
    )
    return jax.shard_map(
        on_device,
        mesh=mesh,
        in_specs=placed,
        out_specs=(P("state", None), P("state", "rank"), P("state", "rank")),
        check_vma=False,
    )
```

```python
import functools

import jax
import jax.numpy as jnp
from jax import lax
from jax.experimental import pallas as pl
from jax.experimental.pallas import tpu as pltpu
from jax.sharding import PartitionSpec as P

MESH = pl.DeviceIdType.MESH
F32 = jnp.float32
BF16 = jnp.bfloat16
GROUP = 8
RANKS = 4
BLOCKS = 2 * RANKS
CHAINS = 4
STEPS = 3


def nn(a, b):
    return lax.dot_general(a, b, (((1,), (0,)), ((), ())), preferred_element_type=F32)


def nt(a, b):
    return lax.dot_general(a, b, (((1,), (1,)), ((), ())), preferred_element_type=F32)


def recursion(
    states_all, zs,
    ids, word_emb, semb, ln, beta, fm, left, right,
    left_o, right_o, bt_o,
    ids_s, ids_v, emb_v, semb_v, ln_v, beta_v, fm_v, u_v, v_v,
    tiles_v, words, w, wn, emit, acc, keep, csm, pb,
    cb, cr, xb, facc, fs1, fr1, fr2, fj, cs, cr1, cr2,
    rs_s, rs_r, ms, mr,
    load, c1s, c1r, xs, xr, c2s, c2r, f1s, f1r, f2s, f2r, f3s, f3r, cs_s, cs_r,
    rss, rsr, ags, agr, mss, msr,
):
    state = lax.axis_index("state")
    y = lax.axis_index("rank")
    chips = zs * GROUP // 2
    g = lax.rem(state, GROUP)
    z = state // GROUP
    chip = state // 2
    core = lax.rem(state, 2)
    yp, yo, ym = lax.rem(y + 1, RANKS), lax.rem(y + 2, RANKS), lax.rem(y + 3, RANKS)
    local, ranks = left.shape
    blk = local // BLOCKS
    hb = w.shape[3]
    half = hb // 2
    batch = CHAINS * hb
    hidden = semb.shape[1]
    count = STEPS * batch

    loads = [
        (ids, ids_s), (ids, ids_v), (word_emb, emb_v), (semb, semb_v), (ln, ln_v), (beta, beta_v), (left, u_v), (fm, fm_v),
    ]
    loads = [pltpu.make_async_copy(src, dst, load.at[k]) for k, (src, dst) in enumerate(loads)]
    ids_l, idv_l, emb_l, semb_l, ln_l, beta_l, u_l, fm_l = loads

    def v_l(j):
        at = pl.ds(pl.multiple_of(j * blk, blk), blk)
        return pltpu.make_async_copy(right.at[at], v_v.at[at], load.at[8 + j])

    for copy in loads[:6] + [v_l(j) for j in range(BLOCKS)] + loads[6:]:
        copy.start()

    def group_peer(d):
        p = lax.rem(g + d, GROUP)
        return p, (z * GROUP + p, y)

    def z_peer(d):
        return (lax.rem(z + d, zs) * GROUP + g, y)

    def chip_peer(d):
        return (2 * lax.rem(chip + d, chips) + core, y)

    partner = (2 * chip + 1 - core, y)
    barrier = pltpu.get_barrier_semaphore()
    greeted = [group_peer(d)[1] for d in range(1, GROUP)] + [(state, other) for other in (yp, yo, ym)]
    for dz in range(1, zs):
        for dx in range(0, GROUP, 2):
            greeted.append((lax.rem(z + dz, zs) * GROUP + lax.rem(g + dx, GROUP), y))
    for who in greeted:
        pl.semaphore_signal(barrier, inc=1, device_id=who, device_id_type=MESH)

    def send(src, dst, send_sem, recv_sem, who):
        pltpu.make_async_remote_copy(
            src_ref=src, dst_ref=dst, send_sem=send_sem, recv_sem=recv_sem, device_id=who, device_id_type=MESH
        ).start()

    def await_bytes(ref, sem):
        pltpu.make_async_copy(ref, ref, sem).wait()

    def each(first, last, act):
        def one(d, carry):
            act(d)
            return carry

        lax.fori_loop(first, last, one, 0, unroll=True)

    def rows(ref, j):
        return ref[pl.ds(pl.multiple_of(j * blk, blk), blk), :]

    lines = ranks // 128

    def columns1():
        def one(j, total):
            return total + nn(jnp.ones((16, blk), BF16), rows(u_v, j))

        total = lax.fori_loop(0, BLOCKS, one, jnp.zeros((16, ranks), F32))
        cs[...] = jnp.zeros_like(cs)
        for c in range(lines):
            cs[0, c:c + 1, :] = total[0:1, 128 * c:128 * c + 128]
        for d in range(1, GROUP):
            send(cs.at[0], cr1.at[d - 1], cs_s.at[0], cs_r.at[0], group_peer(d)[1])

    def columns2():
        await_bytes(cr1, cs_r.at[0])
        total = cs[0]
        for d in range(GROUP - 1):
            total += cr1[d]
        cs[1] = total
        for d in range(1, zs):
            send(cs.at[1], cr2.at[d - 1], cs_s.at[1], cs_r.at[1], z_peer(d))

    def columns3():
        await_bytes(cr2, cs_r.at[1])
        total = cs[1]
        for d in range(zs - 1):
            total += cr2[d]
        line = jnp.concatenate([total[c:c + 1] for c in range(lines)], axis=1)
        high = line.astype(BF16)
        rest = line - high.astype(F32)
        mid = rest.astype(BF16)
        low = (rest - mid.astype(F32)).astype(BF16)
        parts = [x.astype(F32) for x in (high, mid, low)] + [jnp.zeros((13, ranks), F32)]
        csm[...] = jnp.concatenate(parts, axis=0).astype(BF16)

    def find_words(t):
        def one(k, carry):
            tiles_v[k] = emb_v[lax.shift_right_logical(ids_s[t, k], 4)]
            return carry

        lax.fori_loop(0, batch, one, 0, unroll=8)
        lane = lax.broadcasted_iota(jnp.int32, (batch, 16 * batch), 1).astype(F32)
        pick = jnp.where(lane == place[:, t:t + 1], 1.0, 0.0).astype(BF16)
        words[t] = nn(pick, tiles_v[...].reshape(16 * batch, hidden)).astype(BF16)

    ids_l.wait()
    idv_l.wait()
    inside = jnp.bitwise_and(ids_v[...], 15) + 16 * lax.broadcasted_iota(jnp.int32, (STEPS, batch), 1)
    place = jnp.concatenate([inside.astype(F32), jnp.zeros((8 - STEPS, batch), F32)], axis=0).T
    emb_l.wait()
    find_words(STEPS - 1)

    semb_l.wait()
    ln_l.wait()
    beta_l.wait()
    eye = jnp.where(
        lax.broadcasted_iota(jnp.int32, (batch, batch), 0) == lax.broadcasted_iota(jnp.int32, (batch, batch), 1), 1.0, 0.0
    ).astype(BF16)

    def first(j, total):
        logits = nt(words[STEPS - 1], rows(semb_v, j))
        em = jnp.exp(logits - ln_v[j])
        wt = (em * nt(eye, rows(beta_v, j))).astype(BF16)
        for h in range(CHAINS):
            w[0, h, j] = wt[h * hb:(h + 1) * hb]
        v_l(j).wait()
        return total + nn(wt, rows(v_v, j))

    total = lax.fori_loop(0, BLOCKS, first, jnp.zeros((batch, ranks), F32), unroll=4)
    for h in range(CHAINS):
        acc[h] = total[h * hb:(h + 1) * hb]

    pl.semaphore_wait(barrier, len(greeted))

    def sum1(i, h):
        cb[i, h] = acc[h, pl.ds(pl.multiple_of(half * (1 - core), half), half), :].astype(BF16)
        send(cb.at[i, h], cr.at[i, h], c1s.at[i, h], c1r.at[i, h], partner)

    def sum2(i, h):
        await_bytes(cr.at[i, h], c1r.at[i, h])
        mine = acc[h, pl.ds(pl.multiple_of(half * core, half), half), :]
        xb[i, h, chip] = (mine + cr[i, h].astype(F32)).astype(BF16)
        mine = xb.at[i, h, chip]
        each(1, chips, lambda d: send(mine, mine, xs.at[i, h], xr.at[i, h], chip_peer(d)))

    def sum3(i, h):
        await_bytes(xb.at[i, h, pl.ds(0, chips - 1)], xr.at[i, h])
        total = xb[i, h, 0].astype(F32)
        for d in range(1, chips):
            total += xb[i, h, d].astype(F32)
        pb[STEPS - 1 - i, h, core] = total.astype(BF16)
        place_of = pb.at[STEPS - 1 - i, h, core]
        send(place_of, place_of, c2s.at[i, h], c2r.at[i, h], partner)

    def fwd1(i, part):
        t = STEPS - 1 - i

        def one(j, total):
            cols = fm_v[pl.ds(pl.multiple_of(j * blk, blk), blk), pl.ds(pl.multiple_of(t * batch, batch), batch)]
            return total + nn(cols.T, rows(u_v, j))

        @pl.when(part == 0)
        def _():
            facc[...] = jnp.zeros_like(facc)

        count = BLOCKS // CHAINS
        total = facc[...]
        for j in range(count):
            total = one(part * count + j, total)
        facc[...] = total

        @pl.when(part == CHAINS - 1)
        def _():
            for p in range(GROUP):
                fs1[i, p] = facc[16 * p:16 * p + 16].astype(BF16)

            def out(d):
                p, who = group_peer(d)
                send(fs1.at[i, p], fr1.at[i, d - 1], f1s.at[i], f1r.at[i], who)

            each(1, GROUP, out)

    def fwd2(i):
        await_bytes(fr1.at[i], f1r.at[i])
        total = fs1[i, g].astype(F32)
        for d in range(GROUP - 1):
            total += fr1[i, d].astype(F32)
        fr2[i, z] = total.astype(BF16)
        for d in range(1, zs):
            send(fr2.at[i, z], fr2.at[i, z], f2s.at[i], f2r.at[i], z_peer(d))

    def fwd3(i):
        t = STEPS - 1 - i
        await_bytes(fr2.at[i, pl.ds(0, zs - 1)], f2r.at[i])
        total = fr2[i, 0].astype(F32)
        for d in range(1, zs):
            total += fr2[i, d].astype(F32)
        fj[t, g] = (total / states_all).astype(BF16)
        each(1, GROUP, lambda d: send(fj.at[t, g], fj.at[t, g], f3s.at[i], f3r.at[i], group_peer(d)[1]))

    def raw(i, h):
        await_bytes(pb.at[STEPS - 1 - i, h, 0], c2r.at[i, h])
        proj = pb[STEPS - 1 - i, h].reshape(hb, ranks)

        for d, who in ((1, yo), (0, yp), (2, ym)):
            for part in range(2):
                rs_s[i, h, d, part] = nt(proj, rows(u_v, 2 * who + part)).astype(BF16)
            send(rs_s.at[i, h, d], rs_r.at[i, h, d], rss.at[i, h], rsr.at[i, h], (state, who))

        pl.when(jnp.logical_and(i == 0, h == 0))(columns3)
        sums = nt(csm[...], proj)
        ms[i, h, 0:1, 0:hb] = sums[0:1] + sums[1:2] + sums[2:3]
        for d, who in enumerate((yp, yo, ym)):
            send(ms.at[i, h], mr.at[i, h, d], mss.at[i, h], msr.at[i, h], (state, who))

    def raw_own(i, h):
        proj = pb[STEPS - 1 - i, h].reshape(hb, ranks)
        for part in range(2):
            keep[h, part] = nt(proj, rows(u_v, 2 * y + part))

    def mass_of(i, h):
        await_bytes(mr.at[i, h], msr.at[i, h])
        mass = ms[i, h] + mr[i, h, 0] + mr[i, h, 1] + mr[i, h, 2]
        return mass.T[0:hb, 0:1] / states_all

    def own(i, h):
        await_bytes(rs_r.at[i, h], rsr.at[i, h])
        mass = mass_of(i, h)
        for part in range(2):
            total = keep[h, part]
            for d in range(RANKS - 1):
                total += rs_r[i, h, d, part].astype(F32)
            new = (total / mass).astype(BF16).astype(F32)
            w[i + 1, h, 2 * y + part] = (emit[i, h, part] * new).astype(BF16)
        shard = w.at[i + 1, h, pl.ds(2 * y, 2)]
        for who in (yo, yp, ym):
            send(shard, shard, ags.at[i, h], agr.at[i, h], (state, who))

    def landed(i, h):
        await_bytes(w.at[i + 1, h, pl.ds(0, 2 * (RANKS - 1))], agr.at[i, h])

    def project(i, h):
        def term(j):
            return nn(w[i, h, j], rows(v_v, j))

        def shard(who):
            return term(2 * who) + term(2 * who + 1)

        total = shard(y)
        landed(i - 1, h)
        acc[h] = total + shard(yp) + shard(yo) + shard(ym)
        sum1(i, h)

    def turn(i):
        t = STEPS - 1 - i

        def one(j, carry):
            both = jnp.concatenate([w[i, h, j] for h in range(CHAINS)], axis=0)
            wn[pl.ds(pl.multiple_of(j * blk, blk), blk), pl.ds(pl.multiple_of(t * batch, batch), batch)] = both.T
            return carry

        lax.fori_loop(0, BLOCKS, one, 0)

    def grad_left():
        proj = pb[...].reshape(count, ranks)

        def one(j, carry):
            at = pl.ds(pl.multiple_of(j * blk, blk), blk)
            left_o[at, :] = (nn(fm_v[at, :], proj) / count).astype(BF16)
            return carry

        lax.fori_loop(0, BLOCKS, one, 0)

    def grad_right():
        for i in range(STEPS):
            await_bytes(fj.at[i, pl.ds(0, GROUP - 1)], f3r.at[i])
        fwd = fj[...].reshape(count, ranks)

        def one(j, carry):
            at = pl.ds(pl.multiple_of(j * blk, blk), blk)
            right_o[at, :] = (nn(wn[at, :], fwd) / count).astype(BF16)
            return carry

        lax.fori_loop(0, BLOCKS, one, 0)

    each(0, CHAINS, lambda h: sum1(0, h))
    u_l.wait()
    columns1()
    sum2(0, 0)

    ms[...] = jnp.zeros_like(ms)
    for t in range(STEPS - 1):
        find_words(t)
    for i in range(STEPS - 1):
        for part in range(2):
            logits = nt(words[STEPS - 2 - i], rows(semb_v, 2 * y + part))
            em = jnp.exp(logits - ln_v[2 * y + part])
            for h in range(CHAINS):
                emit[i, h, part] = em[h * hb:(h + 1) * hb]
    emit[STEPS - 1] = jnp.ones_like(emit[STEPS - 1])
    columns2()
    sum2(0, 1)
    fm_l.wait()
    lax.fori_loop(0, CHAINS, lambda k, carry: (fwd1(0, k), carry)[1], 0)
    sum3(0, 0)

    def turn_of(n, carry):
        i, k = n // CHAINS, n % CHAINS
        i2, k2 = (n + 2) // CHAINS, (n + 2) % CHAINS
        i3, k3 = (n + 1) // CHAINS, (n + 1) % CHAINS
        more = i2 < STEPS
        raw(i, k)
        pl.when(i < STEPS - 1)(lambda: fwd1(i + 1, k))

        @pl.when(n >= 1)
        def _():
            own((n - 1) // CHAINS, (n - 1) % CHAINS)

        raw_own(i, k)
        pl.when(k == 0)(lambda: fwd2(i))
        pl.when(k == 1)(lambda: fwd3(i))
        pl.when(k == 2)(lambda: turn(i))

        @pl.when(jnp.logical_and(n >= 2, more))
        def _():
            project(i2, k2)

        pl.when(more)(lambda: sum2(i2, k2))
        pl.when(i3 < STEPS)(lambda: sum3(i3, k3))
        pl.when(n == CHAINS * STEPS - 1)(grad_right)
        return carry

    lax.fori_loop(0, CHAINS * STEPS, turn_of, 0)
    own(STEPS - 1, CHAINS - 1)
    grad_left()

    for k in range(2):
        await_bytes((cr1, cr2)[k], cs_s.at[k])

    def shard_left(i, h):
        await_bytes(w.at[i + 1, h, pl.ds(0, 2 * (RANKS - 1))], ags.at[i, h])

    def left_all(i, carry):
        await_bytes(fr1.at[i], f1s.at[i])
        await_bytes(fr2.at[i, pl.ds(0, zs - 1)], f2s.at[i])
        await_bytes(fj.at[i, pl.ds(0, GROUP - 1)], f3s.at[i])
        def chain(h):
            await_bytes(cr.at[i, h], c1s.at[i, h])
            await_bytes(xb.at[i, h, pl.ds(0, chips - 1)], xs.at[i, h])
            await_bytes(pb.at[i, h, 0], c2s.at[i, h])
            await_bytes(mr.at[i, h], mss.at[i, h])
            await_bytes(rs_r.at[i, h], rss.at[i, h])
            pl.when(jnp.logical_or(i < STEPS - 1, h < CHAINS - 1))(lambda: shard_left(i, h))

        each(0, CHAINS, chain)
        return carry

    lax.fori_loop(0, STEPS, left_all, 0)

    for h in range(CHAINS):
        landed(STEPS - 1, h)
        bt_o[h] = w[STEPS, h]
    shard_left(STEPS - 1, CHAINS - 1)


def finish(bt, left, right, beta_o, left_o, right_o, beta_v, sems):
    copies = [pltpu.make_async_copy(left, left_o, sems.at[0]), pltpu.make_async_copy(right, right_o, sems.at[1])]
    for copy in copies:
        copy.start()
    blk = bt.shape[3]

    def one(j, carry):
        both = jnp.concatenate([bt[h, j] for h in range(CHAINS)], axis=0)
        beta_v[pl.ds(pl.multiple_of(j * blk, blk), blk), :] = both.T
        return carry

    lax.fori_loop(0, BLOCKS, one, 0)
    copies.append(pltpu.make_async_copy(beta_v, beta_o, sems.at[2]))
    copies[2].start()
    for copy in copies:
        copy.wait()


def on_device(token_ids, word_emb, state_emb, log_norm, beta_last, forward_marg, trans_left, trans_right):
    states_n = lax.axis_size("state")
    zs = states_n // GROUP
    chips = states_n // 2
    local, hidden = state_emb.shape
    states_all = states_n * local
    vocab = word_emb.shape[0]
    ranks = trans_left.shape[1]
    batch = beta_last.shape[1]
    hb = batch // CHAINS
    blk = local // BLOCKS
    dma = pltpu.SemaphoreType.DMA
    vm = pltpu.VMEM
    scratch = [
        pltpu.SMEM((STEPS, batch), jnp.int32), vm((STEPS, batch), jnp.int32), vm((vocab // 16, 16, hidden), BF16),
        vm((local, hidden), BF16), vm((BLOCKS, 1, blk), F32), vm((local, batch), BF16), vm((local, STEPS * batch), BF16),
        vm((local, ranks), BF16), vm((local, ranks), BF16),
        vm((batch, 16, hidden), BF16), vm((STEPS, batch, hidden), BF16), vm((STEPS + 1, CHAINS, BLOCKS, hb, blk), BF16),
        vm((local, STEPS * batch), BF16), vm((STEPS, CHAINS, 2, hb, blk), F32), vm((CHAINS, hb, ranks), F32),
        vm((CHAINS, 2, hb, blk), F32), vm((16, ranks), BF16), vm((STEPS, CHAINS, 2, hb // 2, ranks), BF16),
        vm((STEPS, CHAINS, hb // 2, ranks), BF16), vm((STEPS, CHAINS, hb // 2, ranks), BF16),
        vm((STEPS, CHAINS, chips, hb // 2, ranks), BF16),
        vm((batch, ranks), F32),
        vm((STEPS, GROUP, 16, ranks), BF16), vm((STEPS, GROUP - 1, 16, ranks), BF16),
        vm((STEPS, zs, 16, ranks), BF16), vm((STEPS, GROUP, 16, ranks), BF16),
        vm((2, 8, 128), F32), vm((GROUP - 1, 8, 128), F32), vm((zs - 1, 8, 128), F32),
        vm((STEPS, CHAINS, RANKS - 1, 2, hb, blk), BF16), vm((STEPS, CHAINS, RANKS - 1, 2, hb, blk), BF16),
        vm((STEPS, CHAINS, 8, 128), F32), vm((STEPS, CHAINS, RANKS - 1, 8, 128), F32),
        dma((8 + BLOCKS,)),
        *[dma((STEPS, CHAINS)) for _ in range(6)], *[dma((STEPS,)) for _ in range(6)], dma((2,)), dma((2,)),
        *[dma((STEPS, CHAINS)) for _ in range(6)],
    ]
    anywhere = pl.BlockSpec(memory_space=pl.ANY)
    inside = pl.BlockSpec(memory_space=pltpu.VMEM)
    left, right, bt = pl.pallas_call(
        functools.partial(recursion, states_all, zs),
        out_shape=(vm((local, ranks), BF16), vm((local, ranks), BF16), vm((CHAINS, BLOCKS, hb, blk), BF16)),
        in_specs=[anywhere] * 8,
        out_specs=[inside] * 3,
        scratch_shapes=scratch,
        compiler_params=pltpu.CompilerParams(
            collective_id=0, has_side_effects=True, vmem_limit_bytes=46 * 2**20
        ),
        name="recursion",
    )(
        token_ids, word_emb.reshape(vocab // 16, 16, hidden), state_emb, log_norm.reshape(BLOCKS, 1, blk), beta_last,
        forward_marg, trans_left, trans_right,
    )
    beta, left, right = pl.pallas_call(
        finish,
        out_shape=(
            jax.ShapeDtypeStruct((local, batch), BF16),
            jax.ShapeDtypeStruct((local, ranks), BF16),
            jax.ShapeDtypeStruct((local, ranks), BF16),
        ),
        in_specs=[inside] * 3,
        out_specs=[anywhere] * 3,
        scratch_shapes=[vm((local, batch), BF16), dma((3,))],
        compiler_params=pltpu.CompilerParams(vmem_limit_bytes=16 * 2**20),
        name="finish",
    )(bt, left, right)
    return beta, left, right


def solution(mesh):
    placed = (
        P(), P(), P("state", None), P("state"), P("state", None), P("state", None), P("state", "rank"), P("state", "rank"),
    )
    return jax.shard_map(
        on_device,
        mesh=mesh,
        in_specs=placed,
        out_specs=(P("state", None), P("state", "rank"), P("state", "rank")),
        check_vma=False,
    )
```

```python
import functools

import jax
import jax.numpy as jnp
from jax import lax
from jax.experimental import pallas as pl
from jax.experimental.pallas import tpu as pltpu
from jax.sharding import PartitionSpec as P

MESH = pl.DeviceIdType.MESH
F32 = jnp.float32
BF16 = jnp.bfloat16
GROUP = 8
RANKS = 4
BLOCKS = 2 * RANKS
CHAINS = 4
STEPS = 3


def nn(a, b):
    return lax.dot_general(a, b, (((1,), (0,)), ((), ())), preferred_element_type=F32)


def nt(a, b):
    return lax.dot_general(a, b, (((1,), (1,)), ((), ())), preferred_element_type=F32)


def recursion(
    states_all, zs,
    ids, word_emb, semb, ln, beta, fm, left, right,
    left_o, right_o, bt_o,
    ids_s, ids_v, emb_v, semb_v, ln_v, beta_v, fm_v, u_v, v_v,
    tiles_v, words, w, wn, emit, acc, keep, csm, pb,
    cb, cr, xb, facc, fs1, fr1, fr2, fj, cs, cr1, cr2,
    rs_s, rs_r, ms, mr,
    load, c1s, c1r, xs, xr, c2s, c2r, f1s, f1r, f2s, f2r, f3s, f3r, cs_s, cs_r,
    rss, rsr, ags, agr, mss, msr,
):
    state = lax.axis_index("state")
    y = lax.axis_index("rank")
    chips = zs * GROUP // 2
    g = lax.rem(state, GROUP)
    z = state // GROUP
    chip = state // 2
    core = lax.rem(state, 2)
    yp, yo, ym = lax.rem(y + 1, RANKS), lax.rem(y + 2, RANKS), lax.rem(y + 3, RANKS)
    local, ranks = left.shape
    blk = local // BLOCKS
    hb = w.shape[3]
    half = hb // 2
    batch = CHAINS * hb
    hidden = semb.shape[1]
    count = STEPS * batch

    loads = [
        (ids, ids_s), (ids, ids_v), (word_emb, emb_v), (semb, semb_v), (ln, ln_v), (beta, beta_v), (left, u_v), (fm, fm_v),
    ]
    loads = [pltpu.make_async_copy(src, dst, load.at[k]) for k, (src, dst) in enumerate(loads)]
    ids_l, idv_l, emb_l, semb_l, ln_l, beta_l, u_l, fm_l = loads

    def v_l(j):
        at = pl.ds(pl.multiple_of(j * blk, blk), blk)
        return pltpu.make_async_copy(right.at[at], v_v.at[at], load.at[8 + j])

    for copy in loads[:6] + [v_l(j) for j in range(BLOCKS)] + loads[6:]:
        copy.start()

    def group_peer(d):
        p = lax.rem(g + d, GROUP)
        return p, (z * GROUP + p, y)

    def z_peer(d):
        return (lax.rem(z + d, zs) * GROUP + g, y)

    def chip_peer(d):
        return (2 * lax.rem(chip + d, chips) + core, y)

    partner = (2 * chip + 1 - core, y)
    barrier = pltpu.get_barrier_semaphore()
    greeted = [group_peer(d)[1] for d in range(1, GROUP)] + [(state, other) for other in (yp, yo, ym)]
    for dz in range(1, zs):
        for dx in range(0, GROUP, 2):
            greeted.append((lax.rem(z + dz, zs) * GROUP + lax.rem(g + dx, GROUP), y))
    for who in greeted:
        pl.semaphore_signal(barrier, inc=1, device_id=who, device_id_type=MESH)

    def send(src, dst, send_sem, recv_sem, who):
        pltpu.make_async_remote_copy(
            src_ref=src, dst_ref=dst, send_sem=send_sem, recv_sem=recv_sem, device_id=who, device_id_type=MESH
        ).start()

    def await_bytes(ref, sem):
        pltpu.make_async_copy(ref, ref, sem).wait()

    def each(first, last, act):
        def one(d, carry):
            act(d)
            return carry

        lax.fori_loop(first, last, one, 0, unroll=True)

    def rows(ref, j):
        return ref[pl.ds(pl.multiple_of(j * blk, blk), blk), :]

    lines = ranks // 128

    def columns1():
        def one(j, total):
            return total + nn(jnp.ones((16, blk), BF16), rows(u_v, j))

        total = lax.fori_loop(0, BLOCKS, one, jnp.zeros((16, ranks), F32))
        cs[...] = jnp.zeros_like(cs)
        for c in range(lines):
            cs[0, c:c + 1, :] = total[0:1, 128 * c:128 * c + 128]
        for d in range(1, GROUP):
            send(cs.at[0], cr1.at[d - 1], cs_s.at[0], cs_r.at[0], group_peer(d)[1])

    def columns2():
        await_bytes(cr1, cs_r.at[0])
        total = cs[0]
        for d in range(GROUP - 1):
            total += cr1[d]
        cs[1] = total
        for d in range(1, zs):
            send(cs.at[1], cr2.at[d - 1], cs_s.at[1], cs_r.at[1], z_peer(d))

    def columns3():
        await_bytes(cr2, cs_r.at[1])
        total = cs[1]
        for d in range(zs - 1):
            total += cr2[d]
        line = jnp.concatenate([total[c:c + 1] for c in range(lines)], axis=1)
        high = line.astype(BF16)
        rest = line - high.astype(F32)
        mid = rest.astype(BF16)
        low = (rest - mid.astype(F32)).astype(BF16)
        parts = [x.astype(F32) for x in (high, mid, low)] + [jnp.zeros((13, ranks), F32)]
        csm[...] = jnp.concatenate(parts, axis=0).astype(BF16)

    def find_words(t):
        def one(k, carry):
            tiles_v[k] = emb_v[lax.shift_right_logical(ids_s[t, k], 4)]
            return carry

        lax.fori_loop(0, batch, one, 0, unroll=8)
        lane = lax.broadcasted_iota(jnp.int32, (batch, 16 * batch), 1).astype(F32)
        pick = jnp.where(lane == place[:, t:t + 1], 1.0, 0.0).astype(BF16)
        words[t] = nn(pick, tiles_v[...].reshape(16 * batch, hidden)).astype(BF16)

    ids_l.wait()
    idv_l.wait()
    inside = jnp.bitwise_and(ids_v[...], 15) + 16 * lax.broadcasted_iota(jnp.int32, (STEPS, batch), 1)
    place = jnp.concatenate([inside.astype(F32), jnp.zeros((8 - STEPS, batch), F32)], axis=0).T
    emb_l.wait()
    find_words(STEPS - 1)

    semb_l.wait()
    ln_l.wait()
    beta_l.wait()
    eye = jnp.where(
        lax.broadcasted_iota(jnp.int32, (batch, batch), 0) == lax.broadcasted_iota(jnp.int32, (batch, batch), 1), 1.0, 0.0
    ).astype(BF16)

    def first(j, total):
        logits = nt(words[STEPS - 1], rows(semb_v, j))
        em = jnp.exp(logits - ln_v[j])
        wt = (em * nt(eye, rows(beta_v, j))).astype(BF16)
        for h in range(CHAINS):
            w[0, h, j] = wt[h * hb:(h + 1) * hb]
        v_l(j).wait()
        return total + nn(wt, rows(v_v, j))

    total = lax.fori_loop(0, BLOCKS, first, jnp.zeros((batch, ranks), F32), unroll=8)
    for h in range(CHAINS):
        acc[h] = total[h * hb:(h + 1) * hb]

    pl.semaphore_wait(barrier, len(greeted))

    def sum1(i, h):
        cb[i, h] = acc[h, pl.ds(pl.multiple_of(half * (1 - core), half), half), :].astype(BF16)
        send(cb.at[i, h], cr.at[i, h], c1s.at[i, h], c1r.at[i, h], partner)

    def sum2(i, h):
        await_bytes(cr.at[i, h], c1r.at[i, h])
        mine = acc[h, pl.ds(pl.multiple_of(half * core, half), half), :]
        xb[i, h, chip] = (mine + cr[i, h].astype(F32)).astype(BF16)
        mine = xb.at[i, h, chip]
        each(1, chips, lambda d: send(mine, mine, xs.at[i, h], xr.at[i, h], chip_peer(d)))

    def sum3(i, h):
        await_bytes(xb.at[i, h, pl.ds(0, chips - 1)], xr.at[i, h])
        total = xb[i, h, 0].astype(F32)
        for d in range(1, chips):
            total += xb[i, h, d].astype(F32)
        pb[STEPS - 1 - i, h, core] = total.astype(BF16)
        place_of = pb.at[STEPS - 1 - i, h, core]
        send(place_of, place_of, c2s.at[i, h], c2r.at[i, h], partner)

    def fwd1(i, part):
        t = STEPS - 1 - i

        def one(j, total):
            cols = fm_v[pl.ds(pl.multiple_of(j * blk, blk), blk), pl.ds(pl.multiple_of(t * batch, batch), batch)]
            return total + nn(cols.T, rows(u_v, j))

        @pl.when(part == 0)
        def _():
            facc[...] = jnp.zeros_like(facc)

        count = BLOCKS // CHAINS
        total = facc[...]
        for j in range(count):
            total = one(part * count + j, total)
        facc[...] = total

        @pl.when(part == CHAINS - 1)
        def _():
            for p in range(GROUP):
                fs1[i, p] = facc[16 * p:16 * p + 16].astype(BF16)

            def out(d):
                p, who = group_peer(d)
                send(fs1.at[i, p], fr1.at[i, d - 1], f1s.at[i], f1r.at[i], who)

            each(1, GROUP, out)

    def fwd2(i):
        await_bytes(fr1.at[i], f1r.at[i])
        total = fs1[i, g].astype(F32)
        for d in range(GROUP - 1):
            total += fr1[i, d].astype(F32)
        fr2[i, z] = total.astype(BF16)
        for d in range(1, zs):
            send(fr2.at[i, z], fr2.at[i, z], f2s.at[i], f2r.at[i], z_peer(d))

    def fwd3(i):
        t = STEPS - 1 - i
        await_bytes(fr2.at[i, pl.ds(0, zs - 1)], f2r.at[i])
        total = fr2[i, 0].astype(F32)
        for d in range(1, zs):
            total += fr2[i, d].astype(F32)
        fj[t, g] = (total / states_all).astype(BF16)
        each(1, GROUP, lambda d: send(fj.at[t, g], fj.at[t, g], f3s.at[i], f3r.at[i], group_peer(d)[1]))

    def raw(i, h):
        await_bytes(pb.at[STEPS - 1 - i, h, 0], c2r.at[i, h])
        proj = pb[STEPS - 1 - i, h].reshape(hb, ranks)

        for d, who in ((1, yo), (0, yp), (2, ym)):
            for part in range(2):
                rs_s[i, h, d, part] = nt(proj, rows(u_v, 2 * who + part)).astype(BF16)
            send(rs_s.at[i, h, d], rs_r.at[i, h, d], rss.at[i, h], rsr.at[i, h], (state, who))

        pl.when(jnp.logical_and(i == 0, h == 0))(columns3)
        sums = nt(csm[...], proj)
        ms[i, h, 0:1, 0:hb] = sums[0:1] + sums[1:2] + sums[2:3]
        for d, who in enumerate((yp, yo, ym)):
            send(ms.at[i, h], mr.at[i, h, d], mss.at[i, h], msr.at[i, h], (state, who))

    def raw_own(i, h):
        proj = pb[STEPS - 1 - i, h].reshape(hb, ranks)
        for part in range(2):
            keep[h, part] = nt(proj, rows(u_v, 2 * y + part))

    def mass_of(i, h):
        await_bytes(mr.at[i, h], msr.at[i, h])
        mass = ms[i, h] + mr[i, h, 0] + mr[i, h, 1] + mr[i, h, 2]
        return mass.T[0:hb, 0:1] / states_all

    def own(i, h):
        await_bytes(rs_r.at[i, h], rsr.at[i, h])
        mass = mass_of(i, h)
        for part in range(2):
            total = keep[h, part]
            for d in range(RANKS - 1):
                total += rs_r[i, h, d, part].astype(F32)
            new = (total / mass).astype(BF16).astype(F32)
            w[i + 1, h, 2 * y + part] = (emit[i, h, part] * new).astype(BF16)
        shard = w.at[i + 1, h, pl.ds(2 * y, 2)]
        for who in (yo, yp, ym):
            send(shard, shard, ags.at[i, h], agr.at[i, h], (state, who))

    def landed(i, h):
        await_bytes(w.at[i + 1, h, pl.ds(0, 2 * (RANKS - 1))], agr.at[i, h])

    def project(i, h):
        def term(j):
            return nn(w[i, h, j], rows(v_v, j))

        def shard(who):
            return term(2 * who) + term(2 * who + 1)

        total = shard(y)
        landed(i - 1, h)
        acc[h] = total + shard(yp) + shard(yo) + shard(ym)
        sum1(i, h)

    def turn(i):
        t = STEPS - 1 - i

        def one(j, carry):
            both = jnp.concatenate([w[i, h, j] for h in range(CHAINS)], axis=0)
            wn[pl.ds(pl.multiple_of(j * blk, blk), blk), pl.ds(pl.multiple_of(t * batch, batch), batch)] = both.T
            return carry

        lax.fori_loop(0, BLOCKS, one, 0)

    def grad_left():
        proj = pb[...].reshape(count, ranks)

        def one(j, carry):
            at = pl.ds(pl.multiple_of(j * blk, blk), blk)
            left_o[at, :] = (nn(fm_v[at, :], proj) / count).astype(BF16)
            return carry

        lax.fori_loop(0, BLOCKS, one, 0)

    def grad_right():
        for i in range(STEPS):
            await_bytes(fj.at[i, pl.ds(0, GROUP - 1)], f3r.at[i])
        fwd = fj[...].reshape(count, ranks)

        def one(j, carry):
            at = pl.ds(pl.multiple_of(j * blk, blk), blk)
            right_o[at, :] = (nn(wn[at, :], fwd) / count).astype(BF16)
            return carry

        lax.fori_loop(0, BLOCKS, one, 0, unroll=2)

    each(0, CHAINS, lambda h: sum1(0, h))
    u_l.wait()
    columns1()
    sum2(0, 0)

    ms[...] = jnp.zeros_like(ms)
    for t in range(STEPS - 1):
        find_words(t)
    for i in range(STEPS - 1):
        for part in range(2):
            logits = nt(words[STEPS - 2 - i], rows(semb_v, 2 * y + part))
            em = jnp.exp(logits - ln_v[2 * y + part])
            for h in range(CHAINS):
                emit[i, h, part] = em[h * hb:(h + 1) * hb]
    emit[STEPS - 1] = jnp.ones_like(emit[STEPS - 1])
    columns2()
    sum2(0, 1)
    fm_l.wait()
    lax.fori_loop(0, CHAINS, lambda k, carry: (fwd1(0, k), carry)[1], 0)
    sum3(0, 0)

    def turn_of(n, carry):
        i, k = n // CHAINS, n % CHAINS
        i2, k2 = (n + 2) // CHAINS, (n + 2) % CHAINS
        i3, k3 = (n + 1) // CHAINS, (n + 1) % CHAINS
        more = i2 < STEPS
        raw(i, k)
        pl.when(i < STEPS - 1)(lambda: fwd1(i + 1, k))

        @pl.when(n >= 1)
        def _():
            own((n - 1) // CHAINS, (n - 1) % CHAINS)

        raw_own(i, k)
        pl.when(k == 0)(lambda: fwd2(i))
        pl.when(k == 1)(lambda: fwd3(i))
        pl.when(k == 2)(lambda: turn(i))

        @pl.when(jnp.logical_and(n >= 2, more))
        def _():
            project(i2, k2)

        pl.when(more)(lambda: sum2(i2, k2))
        pl.when(i3 < STEPS)(lambda: sum3(i3, k3))
        pl.when(n == CHAINS * STEPS - 1)(grad_right)
        return carry

    lax.fori_loop(0, CHAINS * STEPS, turn_of, 0)
    own(STEPS - 1, CHAINS - 1)
    grad_left()

    for k in range(2):
        await_bytes((cr1, cr2)[k], cs_s.at[k])

    def shard_left(i, h):
        await_bytes(w.at[i + 1, h, pl.ds(0, 2 * (RANKS - 1))], ags.at[i, h])

    def left_all(i, carry):
        await_bytes(fr1.at[i], f1s.at[i])
        await_bytes(fr2.at[i, pl.ds(0, zs - 1)], f2s.at[i])
        await_bytes(fj.at[i, pl.ds(0, GROUP - 1)], f3s.at[i])
        def chain(h):
            await_bytes(cr.at[i, h], c1s.at[i, h])
            await_bytes(xb.at[i, h, pl.ds(0, chips - 1)], xs.at[i, h])
            await_bytes(pb.at[i, h, 0], c2s.at[i, h])
            await_bytes(mr.at[i, h], mss.at[i, h])
            await_bytes(rs_r.at[i, h], rss.at[i, h])
            pl.when(jnp.logical_or(i < STEPS - 1, h < CHAINS - 1))(lambda: shard_left(i, h))

        each(0, CHAINS, chain)
        return carry

    lax.fori_loop(0, STEPS, left_all, 0)

    for h in range(CHAINS):
        landed(STEPS - 1, h)
        bt_o[h] = w[STEPS, h]
    shard_left(STEPS - 1, CHAINS - 1)


def finish(bt, left, right, beta_o, left_o, right_o, beta_v, sems):
    copies = [pltpu.make_async_copy(left, left_o, sems.at[0]), pltpu.make_async_copy(right, right_o, sems.at[1])]
    for copy in copies:
        copy.start()
    blk = bt.shape[3]

    def one(j, carry):
        both = jnp.concatenate([bt[h, j] for h in range(CHAINS)], axis=0)
        beta_v[pl.ds(pl.multiple_of(j * blk, blk), blk), :] = both.T
        return carry

    lax.fori_loop(0, BLOCKS, one, 0)
    copies.append(pltpu.make_async_copy(beta_v, beta_o, sems.at[2]))
    copies[2].start()
    for copy in copies:
        copy.wait()


def on_device(token_ids, word_emb, state_emb, log_norm, beta_last, forward_marg, trans_left, trans_right):
    states_n = lax.axis_size("state")
    zs = states_n // GROUP
    chips = states_n // 2
    local, hidden = state_emb.shape
    states_all = states_n * local
    vocab = word_emb.shape[0]
    ranks = trans_left.shape[1]
    batch = beta_last.shape[1]
    hb = batch // CHAINS
    blk = local // BLOCKS
    dma = pltpu.SemaphoreType.DMA
    vm = pltpu.VMEM
    scratch = [
        pltpu.SMEM((STEPS, batch), jnp.int32), vm((STEPS, batch), jnp.int32), vm((vocab // 16, 16, hidden), BF16),
        vm((local, hidden), BF16), vm((BLOCKS, 1, blk), F32), vm((local, batch), BF16), vm((local, STEPS * batch), BF16),
        vm((local, ranks), BF16), vm((local, ranks), BF16),
        vm((batch, 16, hidden), BF16), vm((STEPS, batch, hidden), BF16), vm((STEPS + 1, CHAINS, BLOCKS, hb, blk), BF16),
        vm((local, STEPS * batch), BF16), vm((STEPS, CHAINS, 2, hb, blk), F32), vm((CHAINS, hb, ranks), F32),
        vm((CHAINS, 2, hb, blk), F32), vm((16, ranks), BF16), vm((STEPS, CHAINS, 2, hb // 2, ranks), BF16),
        vm((STEPS, CHAINS, hb // 2, ranks), BF16), vm((STEPS, CHAINS, hb // 2, ranks), BF16),
        vm((STEPS, CHAINS, chips, hb // 2, ranks), BF16),
        vm((batch, ranks), F32),
        vm((STEPS, GROUP, 16, ranks), BF16), vm((STEPS, GROUP - 1, 16, ranks), BF16),
        vm((STEPS, zs, 16, ranks), BF16), vm((STEPS, GROUP, 16, ranks), BF16),
        vm((2, 8, 128), F32), vm((GROUP - 1, 8, 128), F32), vm((zs - 1, 8, 128), F32),
        vm((STEPS, CHAINS, RANKS - 1, 2, hb, blk), BF16), vm((STEPS, CHAINS, RANKS - 1, 2, hb, blk), BF16),
        vm((STEPS, CHAINS, 8, 128), F32), vm((STEPS, CHAINS, RANKS - 1, 8, 128), F32),
        dma((8 + BLOCKS,)),
        *[dma((STEPS, CHAINS)) for _ in range(6)], *[dma((STEPS,)) for _ in range(6)], dma((2,)), dma((2,)),
        *[dma((STEPS, CHAINS)) for _ in range(6)],
    ]
    anywhere = pl.BlockSpec(memory_space=pl.ANY)
    inside = pl.BlockSpec(memory_space=pltpu.VMEM)
    left, right, bt = pl.pallas_call(
        functools.partial(recursion, states_all, zs),
        out_shape=(vm((local, ranks), BF16), vm((local, ranks), BF16), vm((CHAINS, BLOCKS, hb, blk), BF16)),
        in_specs=[anywhere] * 8,
        out_specs=[inside] * 3,
        scratch_shapes=scratch,
        compiler_params=pltpu.CompilerParams(
            collective_id=0, has_side_effects=True, vmem_limit_bytes=46 * 2**20
        ),
        name="recursion",
    )(
        token_ids, word_emb.reshape(vocab // 16, 16, hidden), state_emb, log_norm.reshape(BLOCKS, 1, blk), beta_last,
        forward_marg, trans_left, trans_right,
    )
    beta, left, right = pl.pallas_call(
        finish,
        out_shape=(
            jax.ShapeDtypeStruct((local, batch), BF16),
            jax.ShapeDtypeStruct((local, ranks), BF16),
            jax.ShapeDtypeStruct((local, ranks), BF16),
        ),
        in_specs=[inside] * 3,
        out_specs=[anywhere] * 3,
        scratch_shapes=[vm((local, batch), BF16), dma((3,))],
        compiler_params=pltpu.CompilerParams(vmem_limit_bytes=16 * 2**20),
        name="finish",
    )(bt, left, right)
    return beta, left, right


def solution(mesh):
    placed = (
        P(), P(), P("state", None), P("state"), P("state", None), P("state", None), P("state", "rank"), P("state", "rank"),
    )
    return jax.shard_map(
        on_device,
        mesh=mesh,
        in_specs=placed,
        out_specs=(P("state", None), P("state", "rank"), P("state", "rank")),
        check_vma=False,
    )
```
